32 devices in a mesh: replica: 8 (over y, x, core), group: 4 (over z).
Axes of the slice: x: 2, y: 2, z: 4, core: 2. Of those that a mesh axis runs over, the one named last changes fastest.
Arguments:
- tokens: bfloat16 [8192, 2048], P(('replica', 'group')), may hold values from -6 to 6
- cotangent: bfloat16 [8192, 2048], P(('replica', 'group')), may hold values from -6 to 6
- lengths: int32 [8, 3], P('replica'), may hold values from 1 to 512, 1024 in all within a row
- packing: int32 [8, 1024], P('replica'), may hold values from 0 to 1023, each once within a row
- attn_gain: float32 [2048], P('group'), may hold values from 0.1 to 1.9
- w_query: bfloat16 [2048, 2048], P('group'), may hold values from -0.125 to 0.125
- w_key_value: bfloat16 [2048, 2, 512], P('group'), may hold values from -0.125 to 0.125
- w_out: bfloat16 [2048, 2048], P('group'), may hold values from -0.75 to 0.75
- mlp_gain: float32 [2048], P('group'), may hold values from 0.1 to 1.9
- w_gate_up: bfloat16 [2048, 2, 8192], P('group'), may hold values from -0.125 to 0.125
- w_down: bfloat16 [8192, 2048], P('group'), may hold values from -0.0625 to 0.0625
Outputs:
- mixed: bfloat16 [8192, 2048], P(('replica', 'group'))
- layer_input_gradient: bfloat16 [8192, 2048], P(('replica', 'group'))
- attn_gain_grad: float32 [2048], P('group')
- w_query_grad: float32 [2048, 2048], P('group')
- w_key_value_grad: float32 [2048, 2, 512], P('group')
- w_out_grad: float32 [2048, 2048], P('group')
- mlp_gain_grad: float32 [2048], P('group')
- w_gate_up_grad: float32 [2048, 2, 8192], P('group')
- w_down_grad: float32 [8192, 2048], P('group')
The draws below stay inside these ranges and needn't reach their ends.
Inputs may be any that keep to these rules, and one draw needn't show every extreme that they name: `lengths`: each row sums to 1024 and its largest entry is exactly 512. `packing`: each row holds every number of 0 to 1023 once.
All inputs are finite; a program needn't handle non-finite values.
Results may differ from the reference program's by a relative error of at most 0.035.
Values may be sent and summed in bfloat16 or wider, within the bound.
No kernel may reach another device: no remote copies, remote signals or barrier semaphores. Data moves between devices by JAX's collectives and lax.ppermute only.
A program may use at most 640 MiB of HBM per device.

```python
import math
import jax
import jax.numpy as jnp
import numpy as np
from jax import lax

D = 2048
HEADS = 32
KV_HEADS = 8
HEAD_DIM = 64
FF = 8192
SEQS = 3
GROUP_TOK = 1024
LONGEST = 512
REPLICAS = 8
TOKENS = 8192


def steps_of(stream_key, dims, shards, least, largest):
    level, own = 1.0, jax.random.fold_in(stream_key, 6)
    for dim, blocks in shards:
        draws = jnp.exp(jax.random.uniform(jax.random.fold_in(own, dim), (blocks,), jnp.float32, least / len(shards), largest / len(shards)))
        level = level * jnp.repeat(draws, dims[dim] // blocks).reshape([-1 if axis == dim else 1 for axis in range(len(dims))])
    return level


def profile(count, total, bound, skew):
    portions = [(1 << 20) // math.isqrt(standing ** skew) + 1 for standing in range(2, count + 1)]
    rest, holding = total - bound - (count - 1), [1] * (count - 1)
    while rest > 0:
        movable = [i for i in range(count - 1) if holding[i] < bound]
        whole, left = sum([portions[i] for i in movable]), rest
        for i in movable:
            more = min(bound - holding[i], max(1, left * portions[i] // whole), rest)
            holding[i] = holding[i] + more
            rest = rest - more
    return np.array([bound] + holding)


def uneven_parts(stream_key, count, total, limit, skew):
    if count == 2:
        one = jax.random.randint(stream_key, (), max(1, total - limit), min(limit, total - 1) + 1)
        return jnp.stack([one, total - one])
    tallies = jnp.asarray(profile(count, total, limit, skew), jnp.int32)
    twos = (count - 1) // 2
    source_of, receiver = tallies[1:1 + 2 * twos:2], tallies[2:2 + 2 * twos:2]
    slack = jnp.minimum(source_of - 1, limit - receiver)
    shifted = jax.random.randint(jax.random.fold_in(stream_key, 1), (twos,), 0, 1 << 20) % (slack + 1)
    tallies = tallies.at[1:1 + 2 * twos:2].set(source_of - shifted).at[2:2 + 2 * twos:2].set(receiver + shifted)
    return tallies[jax.random.permutation(jax.random.fold_in(stream_key, 2), count)]


def centred(key, extent, spread, reach, shards=(), kind=jnp.bfloat16):
    result = jax.random.normal(key, extent, jnp.float32) * spread
    if len(shards) > 0:
        result = steps_of(key, extent, shards, -0.22, 0.18) * result
    return jnp.clip(result, min=-reach, max=reach).astype(kind)


def setup_inputs(seed: int = 0) -> dict:
    keys = jax.random.split(jax.random.key(seed), 12)
    tokens = centred(keys[0], (TOKENS, D), 1.0, 6.0, ((0, 32),))
    cotangent = centred(keys[1], (TOKENS, D), 1.0, 6.0, ((0, 32),))
    lengths = jax.vmap(lambda own: uneven_parts(own, SEQS, GROUP_TOK, LONGEST, 2))(jax.random.split(keys[2], REPLICAS)).reshape((REPLICAS, SEQS)).astype(jnp.int32)
    packing = jax.vmap(lambda own: jax.random.permutation(own, GROUP_TOK))(jax.random.split(keys[3], REPLICAS)).reshape((REPLICAS, GROUP_TOK)).astype(jnp.int32)
    attn_gain = jnp.clip(1.0 + 0.18 * jax.random.normal(keys[4], (D,), jnp.float32), 0.1, 1.9)
    w_query = centred(keys[5], (D, HEADS * HEAD_DIM), D ** -0.5, 0.125, ((0, 4),))
    w_key_value = centred(keys[6], (D, 2, KV_HEADS * HEAD_DIM), D ** -0.5, 0.125, ((0, 4),))
    w_out = centred(keys[7], (HEADS * HEAD_DIM, D), (max(HEADS * HEAD_DIM // 32, 1)) ** -0.5, 0.75, ((0, 4),))
    mlp_gain = jnp.clip(1.0 + 0.18 * jax.random.normal(keys[8], (D,), jnp.float32), 0.1, 1.9)
    w_gate_up = centred(keys[9], (D, 2, FF), D ** -0.5, 0.125, ((0, 4),))
    w_down = centred(keys[10], (FF, D), FF ** -0.5, 0.0625, ((0, 4),))
    return {"tokens": tokens, "cotangent": cotangent, "lengths": lengths, "packing": packing, "attn_gain": attn_gain, "w_query": w_query, "w_key_value": w_key_value, "w_out": w_out, "mlp_gain": mlp_gain, "w_gate_up": w_gate_up, "w_down": w_down}


EPS = 1e-05
NEG = -1e+30
HIGH = lax.Precision.HIGHEST

@jax.custom_vjp
def low(v):
    return lax.optimization_barrier(v.astype(jnp.bfloat16)).astype(jnp.float32)

@jax.custom_vjp
def low_back(v):
    return v

def low_keep(v):
    return (low(v), None)

def low_pass(kept, grad):
    return (grad,)

def back_keep(v):
    return (v, None)

def back_low(kept, grad):
    return (low(grad),)
low.defvjp(low_keep, low_pass)
low_back.defvjp(back_keep, back_low)

def frequencies(head_size):
    half = head_size // 2
    expo = jnp.arange(half).astype(jnp.float32) * (2.0 / head_size)
    base = jnp.power(jnp.float32(500000.0), -expo)
    wavelen = 2.0 * math.pi / base
    smooth = (8192.0 / wavelen - 1.0) / 3.0
    middle = (1.0 - smooth) * base / 32.0 + smooth * base
    return jnp.where(wavelen < 2048.0, base, jnp.where(wavelen > 8192.0, base / 32.0, middle))

def stream_meta(lengths_row, stream):
    ends = jnp.cumsum(lengths_row).astype(jnp.int32)
    past = ends[None, :] <= stream[:, None]
    segment = lax.optimization_barrier(jnp.sum(past.astype(jnp.int32), axis=1)).astype(jnp.int32)
    before = lax.optimization_barrier(jnp.sum(jnp.where(past, lengths_row[None, :], 0), axis=1)).astype(jnp.int32)
    return (segment, (stream - before).astype(jnp.int32))

def rope(value, cosine, sine):
    half = value.shape[-1] // 2
    first, second = (value[..., :half], value[..., half:])
    return jnp.concatenate([first * cosine - second * sine, second * cosine + first * sine], axis=-1)

def rms_normalize_rows(value):
    return value * lax.rsqrt(lax.optimization_barrier(jnp.mean(value * value, axis=-1, keepdims=True)) + EPS)

def group_forward(weights, x, lengths_row, packing_row):
    w_query, w_key_value, w_out, attn_gain, w_gate_up, w_down, mlp_gain = weights
    segment, position = stream_meta(lengths_row, packing_row)
    ntok = x.shape[0]
    share = HEADS // KV_HEADS
    angles = position.astype(jnp.float32)[:, None] * frequencies(HEAD_DIM)[None, :]
    cosine = jnp.cos(angles)[:, None, :]
    sine = jnp.sin(angles)[:, None, :]
    normed = low(rms_normalize_rows(x) * attn_gain)
    query = low_back(jnp.dot(normed, w_query, precision=HIGH))
    keyval = low_back(jnp.einsum('tc,cjk->tjk', normed, w_key_value, precision=HIGH))
    q_rot = low(rope(query.reshape(ntok, HEADS, HEAD_DIM), cosine, sine))
    q_rot = q_rot.reshape(ntok, KV_HEADS, share, HEAD_DIM)
    k_rot = low(rope(keyval[:, 0].reshape(ntok, KV_HEADS, HEAD_DIM), cosine, sine))
    values = low(keyval[:, 1].reshape(ntok, KV_HEADS, HEAD_DIM))
    block = min(512, ntok)
    nblock = ntok // block

    @jax.checkpoint
    def attend(item):
        q_block, seg_q, pos_q = item
        raw = jnp.einsum('tkgd,skd->kgts', q_block, k_rot, precision=HIGH) * HEAD_DIM ** (-0.5)
        scores = low_back(raw)
        mask = (seg_q[:, None] == segment[None, :]) & (position[None, :] <= pos_q[:, None])
        masked = jnp.where(mask, scores, NEG)
        top = lax.optimization_barrier(jnp.max(masked, axis=-1, keepdims=True))
        total = lax.optimization_barrier(jnp.sum(jnp.where(mask, jnp.exp(masked - top), 0.0), axis=-1, keepdims=True))
        lse = top + jnp.log(total)
        probs = low(jnp.where(mask, jnp.exp(masked - lse), 0.0))
        return jnp.einsum('kgts,skd->tkgd', probs, values, precision=HIGH)
    heads_out = lax.map(attend, (q_rot.reshape(nblock, block, KV_HEADS, share, HEAD_DIM), segment.reshape(nblock, block), position.reshape(nblock, block)))
    attended = low(low_back(heads_out.reshape(ntok, HEADS * HEAD_DIM)))
    residual_after_attention = x + low_back(jnp.dot(attended, w_out, precision=HIGH))
    second_normalized_rows = low(rms_normalize_rows(residual_after_attention) * mlp_gain)
    gateup = low_back(jnp.einsum('tc,cjf->tjf', second_normalized_rows, w_gate_up, precision=HIGH))
    hidden = low(jax.nn.silu(gateup[:, 0]) * gateup[:, 1])
    return residual_after_attention + low_back(jnp.dot(hidden, w_down, precision=HIGH))

def reference(tokens, cotangent, lengths, packing, attn_gain, w_query, w_key_value, w_out, mlp_gain, w_gate_up, w_down):
    weights = (w_query.astype(jnp.float32), w_key_value.astype(jnp.float32), w_out.astype(jnp.float32), attn_gain.astype(jnp.float32), w_gate_up.astype(jnp.float32), w_down.astype(jnp.float32), mlp_gain.astype(jnp.float32))
    inputs = tokens.astype(jnp.float32).reshape(REPLICAS, GROUP_TOK, D)

    def forward(weights, inputs):

        def step(carry, item):
            hidden_input_rows, lengths_row, packing_row = item
            return (carry, jax.checkpoint(group_forward)(weights, hidden_input_rows, lengths_row, packing_row))
        _, outputs = lax.scan(step, jnp.zeros((), jnp.float32), (inputs, lengths, packing))
        return outputs
    outputs, pull = jax.vjp(forward, weights, inputs)
    grads, input_grads = pull(cotangent.astype(jnp.float32).reshape(REPLICAS, GROUP_TOK, D))
    g_query, g_keyval, g_out, g_attn_gain, g_gate_up, g_down, g_mlp_gain = grads
    mixed = outputs.reshape(TOKENS, D).astype(jnp.bfloat16)
    layer_input_gradient = input_grads.reshape(TOKENS, D).astype(jnp.bfloat16)
    return (mixed, layer_input_gradient, g_attn_gain, g_query, g_keyval, g_out, g_mlp_gain, g_gate_up, g_down)
```

```python
import functools
import math

import jax
import jax.numpy as jnp
from jax import lax
from jax.experimental import pallas as pl
from jax.experimental.pallas import tpu as pltpu
from jax.sharding import PartitionSpec as P

HEADS = 32
KV_HEADS = 8
HEAD_DIM = 64
EPS = 1e-05
NEG = -1e30
F32 = jnp.float32
BF16 = jnp.bfloat16
LIGHT = pl.CostEstimate(flops=1, bytes_accessed=1, transcendentals=0)
HEAVY = pl.CostEstimate(flops=3 * 10**11, bytes_accessed=1, transcendentals=0)


def frequencies(head_size):
    half = head_size // 2
    expo = jnp.arange(half).astype(F32) * (2.0 / head_size)
    base = jnp.power(F32(500000.0), -expo)
    wavelen = 2.0 * math.pi / base
    smooth = (8192.0 / wavelen - 1.0) / 3.0
    middle = (1.0 - smooth) * base / 32.0 + smooth * base
    return jnp.where(wavelen < 2048.0, base, jnp.where(wavelen > 8192.0, base / 32.0, middle))


def stream_meta(lengths_row, stream):
    ends = jnp.cumsum(lengths_row)
    past = ends[None, :] <= stream[:, None]
    segment = jnp.sum(past.astype(jnp.int32), axis=1)
    before = jnp.sum(jnp.where(past, lengths_row[None, :], 0), axis=1)
    return (segment, stream - before)


def inverse_rms(value):
    return lax.rsqrt(jnp.mean(value * value, axis=-1, keepdims=True) + EPS)


def rms_norm_backward(grad, unit, inverse, gain):
    scaled = grad * gain
    return inverse * (scaled - unit * jnp.mean(scaled * unit, axis=-1, keepdims=True))


def swap_halves(value):
    wide = value.shape[-1]
    lane = lax.broadcasted_iota(jnp.int32, value.shape, 1)
    low = lane % HEAD_DIM < HEAD_DIM // 2
    return jnp.where(
        low,
        pltpu.roll(value, wide - HEAD_DIM // 2, 1),
        pltpu.roll(value, HEAD_DIM // 2, 1),
    )


def rotate(value, cosine, sine, width):
    copies = value.shape[-1] // cosine.shape[-1]
    cosine = jnp.concatenate([cosine] * copies, axis=1)
    sine = jnp.concatenate([sine] * copies, axis=1)
    lane = lax.broadcasted_iota(jnp.int32, value.shape, 1)
    return jnp.where(lane < width, value * cosine + swap_halves(value) * sine, value)


def dot(left, right, dims):
    return lax.dot_general(left, right, (dims, ((), ())), preferred_element_type=F32)


def stacked(ref, rows, first, share):
    return jnp.concatenate(
        [ref[rows, (first + h) * HEAD_DIM : (first + h + 1) * HEAD_DIM] for h in range(share)], axis=0
    )


def bias_of(start, row0, block, keys):
    row = row0 + lax.broadcasted_iota(jnp.int32, (block, keys), 0)
    col = lax.broadcasted_iota(jnp.int32, (block, keys), 1)
    return jnp.where((col <= row) & (col >= start), 0.0, NEG).astype(F32)


def forward_kernel(
    hl, kvl, block, qkv_ref, cos_ref, sin_ref, start_ref, place_ref,
    q_ref, k_ref, v_ref, att_ref, lse_ref, low_ref,
):
    total = qkv_ref.shape[0]
    share = hl // kvl
    qw, kw = hl * HEAD_DIM, kvl * HEAD_DIM
    for row0 in range(0, total, block):
        rows = pl.ds(row0, block)
        turned = rotate(qkv_ref[rows, :], cos_ref[rows, :], sin_ref[rows, :], qw + kw)
        q_ref[rows, :] = (turned[:, :qw].astype(BF16) * HEAD_DIM ** (-0.5)).astype(BF16)
        k_ref[rows, :] = turned[:, qw : qw + kw].astype(BF16)
        v_ref[rows, :] = turned[:, qw + kw :].astype(BF16)
    for row0 in range(0, total, block):
        rows = pl.ds(row0, block)
        keys = row0 + block
        bias = bias_of(start_ref[rows, :], row0, block, keys)
        for kv in range(kvl):
            cols = slice(kv * HEAD_DIM, (kv + 1) * HEAD_DIM)
            query = stacked(q_ref, rows, kv * share, share)
            raw = dot(query, k_ref[:keys, cols], ((1,), (1,)))
            raw = (raw.reshape(share, block, keys) + bias[None]).reshape(share * block, keys)
            top = jnp.max(raw, axis=-1, keepdims=True)
            probs = jnp.exp(raw - top)
            total_p = jnp.sum(probs, axis=-1, keepdims=True)
            out = dot(probs.astype(BF16), v_ref[:keys, cols], ((1,), (0,))) / total_p
            lse = top + jnp.log(total_p)
            for h in range(share):
                head = kv * share + h
                part = slice(h * block, (h + 1) * block)
                att_ref[rows, head * HEAD_DIM : (head + 1) * HEAD_DIM] = out[part]
                lse_ref[rows, head : head + 1] = lse[part]
    low_ref[...] = dot(place_ref[...], att_ref[...].astype(BF16), ((0,), (0,))).astype(BF16)


def backward_kernel(
    hl, kvl, block, q_ref, k_ref, v_ref, att_ref, lse_ref, heads_ref, cos_ref, sin_ref, start_ref, place_ref,
    grad_ref, native_ref, gh_ref, gq_ref, gk_ref, gv_ref,
):
    total = q_ref.shape[0]
    share = hl // kvl
    qw, kw = hl * HEAD_DIM, kvl * HEAD_DIM
    gh_ref[...] = dot(place_ref[...], heads_ref[...], ((1,), (0,))).astype(BF16)
    gk_ref[...] = jnp.zeros_like(gk_ref)
    gv_ref[...] = jnp.zeros_like(gv_ref)
    for row0 in range(0, total, block):
        rows = pl.ds(row0, block)
        keys = row0 + block
        bias = bias_of(start_ref[rows, :], row0, block, keys)
        for kv in range(kvl):
            cols = slice(kv * HEAD_DIM, (kv + 1) * HEAD_DIM)
            query = stacked(q_ref, rows, kv * share, share)
            heads = stacked(gh_ref, rows, kv * share, share)
            att = stacked(att_ref, rows, kv * share, share)
            delta = jnp.sum(heads.astype(F32) * att, axis=-1, keepdims=True)
            lse = jnp.concatenate(
                [lse_ref[rows, kv * share + h : kv * share + h + 1] for h in range(share)], axis=0
            )
            raw = dot(query, k_ref[:keys, cols], ((1,), (1,)))
            raw = (raw.reshape(share, block, keys) + bias[None]).reshape(share * block, keys)
            probs = jnp.exp(raw - lse)
            grad_probs = dot(heads, v_ref[:keys, cols], ((1,), (1,)))
            scores = (probs * (grad_probs - delta)).astype(BF16)
            out = dot(scores, k_ref[:keys, cols], ((1,), (0,))) * HEAD_DIM ** (-0.5)
            for h in range(share):
                head = kv * share + h
                gq_ref[rows, head * HEAD_DIM : (head + 1) * HEAD_DIM] = out[h * block : (h + 1) * block]
            gk_ref[:keys, cols] += dot(scores, query, ((0,), (0,)))
            gv_ref[:keys, cols] += dot(probs.astype(BF16), heads, ((0,), (0,)))
    for row0 in range(0, total, block):
        rows = pl.ds(row0, block)
        grad = jnp.concatenate([gq_ref[rows, :], gk_ref[rows, :], gv_ref[rows, :]], axis=1)
        grad_ref[rows, :] = rotate(grad, cos_ref[rows, :], -sin_ref[rows, :], qw + kw).astype(BF16)
    native_ref[...] = dot(place_ref[...], grad_ref[...], ((0,), (0,))).astype(BF16)


def vmem(count):
    return [pl.BlockSpec(memory_space=pltpu.VMEM)] * count


def attention_forward(hl, kvl, qkv, cosine, sine, start, place):
    total = qkv.shape[0]
    block = 256 if total <= 1024 else 128
    qw, kw = hl * HEAD_DIM, kvl * HEAD_DIM
    shape = jax.ShapeDtypeStruct
    return pl.pallas_call(
        functools.partial(forward_kernel, hl, kvl, block),
        out_shape=(
            shape((total, qw), BF16), shape((total, kw), BF16), shape((total, kw), BF16),
            shape((total, qw), F32), shape((total, 128), F32), shape((total, qw), BF16),
        ),
        in_specs=vmem(5), out_specs=tuple(vmem(6)),
        compiler_params=pltpu.CompilerParams(
            vmem_limit_bytes=(32 if total <= 1024 else 56) * 2**20
        ),
        cost_estimate=LIGHT,
        name="attention_forward",
    )(qkv, cosine, sine, start, place)


def attention_backward(hl, kvl, q, k, v, att, lse, heads, cosine, sine, start, place):
    total = q.shape[0]
    block = 256 if total <= 1024 else 128
    qw, kw = hl * HEAD_DIM, kvl * HEAD_DIM
    shape = jax.ShapeDtypeStruct
    return pl.pallas_call(
        functools.partial(backward_kernel, hl, kvl, block),
        out_shape=(shape((total, qw + 2 * kw), BF16), shape((total, qw + 2 * kw), BF16)),
        in_specs=vmem(10), out_specs=tuple(vmem(2)),
        scratch_shapes=[
            pltpu.VMEM((total, qw), BF16), pltpu.VMEM((total, qw), F32),
            pltpu.VMEM((total, kw), F32), pltpu.VMEM((total, kw), F32),
        ],
        compiler_params=pltpu.CompilerParams(
            vmem_limit_bytes=(44 if total <= 1024 else 56) * 2**20
        ),
        cost_estimate=HEAVY,
        name="attention_backward",
    )(q, k, v, att, lse, heads, cosine, sine, start, place)


def hidden_kernel(
    parts, n2_ref, dy_ref, up_ref, down_ref, hidden_ref, gate_grad_ref, up_grad_ref, grad_ref, grad_sum
):
    step = pl.program_id(0)
    wide = down_ref.shape[0] // parts
    total = None
    for part in range(parts):
        cols = slice(part * wide, (part + 1) * wide)
        both = dot(n2_ref[...], up_ref[part], ((1,), (0,)))
        gate, up = both[:, :wide], both[:, wide:]
        grad = dot(dy_ref[...], down_ref[cols, :], ((1,), (1,)))
        sigma = 1.0 / (1.0 + jnp.exp(-gate))
        silu = gate * sigma
        hidden_ref[:, cols] = (silu * up).astype(BF16)
        grad_gate = (grad * up * sigma * (1.0 + gate * (1.0 - sigma))).astype(BF16)
        grad_up = (grad * silu).astype(BF16)
        gate_grad_ref[:, cols] = grad_gate
        up_grad_ref[:, cols] = grad_up
        both = jnp.concatenate([grad_gate, grad_up], axis=1)
        both = dot(both, up_ref[part], ((1,), (1,)))
        total = both if total is None else total + both

    @pl.when(step == 0)
    def _():
        grad_sum[...] = total

    @pl.when(step > 0)
    def _():
        grad_sum[...] += total

    @pl.when(step == pl.num_programs(0) - 1)
    def _():
        grad_ref[...] = grad_sum[...].astype(BF16)


def feed_forward(n2, dy, w_gu, w_down):
    rows, width = n2.shape
    ffs = w_down.shape[0]
    count, _, both = w_gu.shape
    wide = both // 2
    parts = max(1, 512 // wide)
    tile = parts * wide
    shape = jax.ShapeDtypeStruct
    whole = pl.BlockSpec((rows, width), lambda j: (0, 0), pipeline_mode=pl.Buffered(1))
    return pl.pallas_call(
        functools.partial(hidden_kernel, parts),
        grid=(count // parts,),
        in_specs=[
            whole,
            whole,
            pl.BlockSpec((parts, width, both), lambda j: (j, 0, 0)),
            pl.BlockSpec((tile, width), lambda j: (j, 0)),
        ],
        out_specs=[pl.BlockSpec((rows, tile), lambda j: (0, j))] * 3 + [whole],
        out_shape=[shape((rows, ffs), BF16)] * 3 + [shape((rows, width), BF16)],
        scratch_shapes=[pltpu.VMEM((rows, width), F32)],
        compiler_params=pltpu.CompilerParams(vmem_limit_bytes=60 * 2**20),
        cost_estimate=LIGHT,
        name="feed_forward",
    )(n2, dy, w_gu, w_down)


def product_kernel(parts, *refs):
    lefts, rights = refs[:parts], refs[parts:-3]
    out_ref, done_ref, turned_ref = refs[-3:]
    count = len(rights) // parts
    step = pl.program_id(1)
    each = pl.num_programs(1) // count
    size = lefts[0].shape[0]

    @pl.when(step == 0)
    def _():
        for part in range(parts):
            turned_ref[:, part * size : (part + 1) * size] = lefts[part][...].T
        done_ref[...] = jnp.zeros_like(done_ref)

    for which in range(count):

        @pl.when((step >= which * each) & (step < (which + 1) * each))
        def _():
            value = 0.0
            for part in range(parts):
                turned = turned_ref[:, part * size : (part + 1) * size]
                value += dot(turned, rights[which * parts + part][...], ((1,), (0,)))
            out_ref[...] = value.astype(BF16).reshape(out_ref.shape)


def weight_gradient(lefts, rights, blocks, replicas, by_block):
    parts, (size, width) = len(lefts), lefts[0].shape
    cols = rights[0][0].shape[1]
    rows = width // blocks
    tile = min(1024, cols)
    each = cols // tile

    def place(which):
        return lambda i, j: (0, jnp.clip(j - which * each, 0, each - 1))

    if by_block:
        shape = (replicas, blocks, rows // replicas, len(rights) * cols)
        out_spec = pl.BlockSpec((replicas, 1, rows // replicas, tile), lambda i, j: (0, i, 0, j))
    else:
        shape = (width, len(rights) * cols)
        out_spec = pl.BlockSpec((rows, tile), lambda i, j: (i, j))
    return pl.pallas_call(
        functools.partial(product_kernel, parts),
        grid=(blocks, len(rights) * each),
        in_specs=[pl.BlockSpec((size, rows), lambda i, j: (0, i))] * parts
        + [pl.BlockSpec((size, tile), place(n)) for n in range(len(rights)) for _ in range(parts)],
        out_specs=[out_spec, pl.BlockSpec((8, 128), lambda i, j: (0, 0))],
        out_shape=[jax.ShapeDtypeStruct(shape, BF16), jax.ShapeDtypeStruct((8, 128), F32)],
        scratch_shapes=[pltpu.VMEM((rows, parts * size), BF16)],
        compiler_params=pltpu.CompilerParams(vmem_limit_bytes=56 * 2**20),
        cost_estimate=LIGHT,
        name="weight_gradient",
    )(*lefts, *[part for right in rights for part in right])


def mark(value):
    while value.ndim > 2:
        value = value[0]
    return value[:8, :128]


def after(value, *others):
    leaves, tree = jax.tree.flatten(value)
    others = [mark(other) for other in jax.tree.leaves(others)]
    anywhere = pl.BlockSpec(memory_space=pl.ANY)
    tied = pl.pallas_call(
        lambda *refs: None,
        out_shape=[jax.ShapeDtypeStruct(leaf.shape, leaf.dtype) for leaf in leaves],
        in_specs=[anywhere] * (len(leaves) + len(others)),
        out_specs=[anywhere] * len(leaves),
        input_output_aliases={i: i for i in range(len(leaves))},
        cost_estimate=LIGHT,
        name="after",
    )(*leaves, *others)
    return jax.tree.unflatten(tree, tied)


class Line:
    def __init__(self, count):
        self.count = count
        self.me = lax.axis_index("group")

    def swap(self, value, slot):
        return lax.ppermute(value, "group", [(i, i ^ slot) for i in range(self.count)])

    def at(self, value, slot, axis=0):
        return lax.dynamic_index_in_dim(value, self.me ^ slot, axis, keepdims=False)

    def exchange(self, slots):
        return [slots[0]] + [self.swap(slots[k], k) for k in range(1, self.count)]

    def ordered(self, slots):
        return [self.pick(slots, j) for j in range(self.count)]

    def pick(self, slots, device):
        value = slots[0]
        for k in range(1, self.count):
            value = jnp.where(self.me == device ^ k, slots[k], value)
        return value

    def near(self, begun):
        low, high = after((begun[0][1], begun[1][1]))
        return jnp.where(self.me % 2 == 0, high, low)

    def gather(self, value, gates=(), hops=None, begun=None):
        count = self.count
        low, high = begun if begun else ([value], [value])
        low, high = list(low), list(high)
        for hop in range(len(low), (hops or count - 1) + 1):
            moving = (low[-1], high[-1])
            if hop <= len(gates) and gates[hop - 1] is not None:
                if hop == 1:
                    moving = (after(value, gates[0]),) * 2
                else:
                    moving = after(moving, gates[hop - 1])
            up = [(i, i + 1) for i in range(hop - 1, count - 1)]
            down = [(i + 1, i) for i in range(count - hop)]
            low.append(lax.ppermute(moving[0], "group", up))
            high.append(lax.ppermute(moving[1], "group", down))
        if hops:
            return low, high
        self.last = (low[1:], high[1:])
        slots = [value]
        for k in range(1, count):
            chosen = None
            for device in range(count):
                source = device ^ k
                came = high[source - device] if source > device else low[device - source]
                chosen = came if chosen is None else jnp.where(self.me == device, came, chosen)
            slots.append(chosen)
        return slots

    def scatter_sum(self, slots):
        count = self.count
        to_up = to_down = None
        self.hops = []
        for hop in range(count - 1, 0, -1):
            up = [(i, i + 1) for i in range(count - hop)]
            down = [(i + 1, i) for i in range(hop - 1, count - 1)]
            mine_up = self.pick_far(slots, hop)
            mine_down = self.pick_far(slots, -hop)
            if to_up is not None:
                mine_up, mine_down = mine_up + to_up, mine_down + to_down
            to_up = lax.ppermute(mine_up, "group", up)
            to_down = lax.ppermute(mine_down, "group", down)
            self.hops.append((to_up, to_down))
        return slots[0].astype(F32) + to_up.astype(F32) + to_down.astype(F32)

    def pick_far(self, slots, distance):
        chosen = slots[1]
        for device in range(self.count):
            other = device + distance
            if 0 <= other < self.count:
                chosen = jnp.where(self.me == device, slots[device ^ other], chosen)
        return chosen


def local(
    tokens,
    cotangent,
    lengths,
    packing,
    attn_gain,
    w_query,
    w_key_value,
    w_out,
    mlp_gain,
    w_gate_up,
    w_down,
):
    ntok, width = tokens.shape
    total = packing.shape[1]
    groups = total // ntok
    shard = w_query.shape[0]
    replicas = lax.axis_size("replica")
    rows = shard // replicas
    kvl = KV_HEADS // groups
    hl = HEADS // groups
    qw = hl * HEAD_DIM
    kw = kvl * HEAD_DIM
    qkvw = qw + 2 * kw
    ff = w_gate_up.shape[2]
    ffs = ff // groups
    me_r = lax.axis_index("replica")
    line = Line(groups)

    def own_rows(value):
        return lax.dynamic_slice_in_dim(value, me_r * rows, rows)

    def over_plane(value):
        return lax.all_gather(value, "replica", axis=0)

    wq_rows = own_rows(w_query).reshape(rows, groups, qw)
    wkv_rows = own_rows(w_key_value).reshape(rows, 2, groups, kw)
    wkv_rows = wkv_rows.transpose(0, 2, 1, 3).reshape(rows, groups, 2 * kw)
    qkv_rows = jnp.concatenate([wq_rows, wkv_rows], axis=2)
    ffr = ffs // replicas
    gu_cols = []
    for k in range(groups):
        first = (line.me ^ k) * ffs + me_r * ffr
        part = lax.dynamic_slice(w_gate_up, (0, 0, first), (shard, 2, ffr))
        gu_cols.append(jnp.concatenate([part[:, 0], part[:, 1]], axis=1))
    gu_cols = jnp.stack(gu_cols)
    out_cols = lax.dynamic_slice_in_dim(w_out, me_r * (width // replicas), width // replicas, 1)

    w_qkv = line.exchange([line.at(qkv_rows, k, 1) for k in range(groups)])
    gains = jnp.stack([attn_gain, mlp_gain])
    gains = jnp.concatenate(line.ordered(line.exchange([gains] * groups)), axis=1)
    gain1, gain2 = gains[0], gains[1]
    w_out_cols = line.exchange([out_cols] * groups)
    x_hops = line.gather(tokens, (), 1)
    x_came = [part[1] for part in x_hops]
    w_qkv, w_out_cols[1:], x_came = after((w_qkv, w_out_cols[1:], x_came), gu_cols)
    x_hops = [[tokens, part] for part in x_came]
    seats = jnp.arange(total, dtype=jnp.int32)
    _, position = stream_meta(lengths[0], seats)
    start = (seats - position)[:, None]
    angles = position.astype(F32)[:, None] * frequencies(HEAD_DIM)[None, :]
    copies = 128 // HEAD_DIM
    cosine = jnp.tile(jnp.cos(angles), (1, 2 * copies))
    sine = jnp.sin(angles)
    sine = jnp.tile(jnp.concatenate([-sine, sine], axis=1), (1, copies))
    seat = packing.reshape(groups, ntok)
    seat = jnp.concatenate([line.at(seat, k) for k in range(groups)])
    place = (seat[None, :] == seats[:, None]).astype(BF16)
    w_qkv = over_plane(jnp.stack(line.ordered(w_qkv)))
    w_qkv = jnp.swapaxes(w_qkv, 0, 1).reshape(width, qkvw)
    x_slots = line.gather(tokens, (), 0, x_hops)
    x_last = [part[-1] for part in line.last]
    w_out_cols = over_plane(jnp.concatenate(w_out_cols))
    gu_cols = after(gu_cols, x_last)
    gu_cols = line.exchange([gu_cols[k] for k in range(groups)])
    dy_hops = line.gather(cotangent, (x_last,), 1)

    def normed(value):
        value = value.astype(F32)
        return (value * inverse_rms(value) * gain1).astype(BF16)

    normed1 = jnp.concatenate([normed(value) for value in x_slots])
    normed1 = dot(place, normed1, ((1,), (0,))).astype(BF16)
    qkv = dot(normed1, w_qkv, ((1,), (0,)))
    q_rot, k_rot, values, attended, lse, attended_low = attention_forward(
        hl, kvl, qkv, cosine, sine, start, place
    )

    def cut(value):
        return [value[k * ntok : (k + 1) * ntok] for k in range(groups)]

    dy_near = dy_hops
    attended_low = after(attended_low, [part[1] for part in dy_hops])
    own_attended = line.exchange(cut(attended_low))
    w_gu = over_plane(jnp.concatenate(line.ordered(after(gu_cols, attended_low))))
    x_own = tokens.astype(F32)
    own_attended_all = jnp.concatenate(own_attended, axis=1)
    h1 = lax.dot_general(own_attended_all, w_out_cols, (((1,), (1,)), ((), ())), preferred_element_type=F32)
    h1 = x_own + h1.reshape(ntok, width)
    inv2 = inverse_rms(h1)
    unit2 = h1 * inv2
    normed2 = (unit2 * gain2).astype(BF16)
    n2_near = line.gather(normed2, (), 1)
    dy_hops = line.gather(cotangent, (None, own_attended[1:]), 2, dy_hops)
    near_parts = [
        jnp.concatenate([own, line.near(begun)])
        for own, begun in ((normed2, n2_near), (cotangent, dy_near))
    ]

    half = groups // 2
    if half > 2:
        n2, dy = line.gather(normed2, (), 0, n2_near), line.gather(cotangent, (), 0, dy_hops)
        near_parts = [jnp.concatenate(part[:half]) for part in (n2, dy)]
    near = feed_forward(*near_parts, w_gu, w_down)
    if half == 2:
        n2 = line.gather(normed2, (None, None, near[3]), 0, n2_near)
        dy = line.gather(cotangent, (None, None, n2_near), 0, dy_hops)
    n2_parts = [near_parts[0], jnp.concatenate(n2[half:])]
    dy_parts = [near_parts[1], jnp.concatenate(dy[half:])]
    n2_parts[1] = after(n2_parts[1], near[3])
    far = feed_forward(n2_parts[1], dy_parts[1], w_gu, w_down)
    grad_n2 = line.exchange(cut(near[3])[:half] + cut(far[3])[:half])

    def sum_plane(value):
        return lax.psum_scatter(value, "replica", scatter_dimension=0)

    hidden = [near[0], far[0]]
    down_grad, down_done = weight_gradient(hidden, [dy_parts], groups, replicas, False)
    n2_parts[0] = after(n2_parts[0], down_done)
    gu_grad, gu_done = weight_gradient(
        n2_parts, [[near[1], far[1]], [near[2], far[2]]], groups, replicas, True
    )
    down_grad = sum_plane(down_grad.reshape(replicas, ffs // replicas, width))
    gu_grad = gu_grad.reshape(replicas, groups * rows, 2 * ffs)
    gu_grad = sum_plane(gu_grad).reshape(groups, rows, 2 * ffs)

    grad_n2 = after(grad_n2, gu_done)
    grad_n2 = sum([part.astype(F32) for part in grad_n2])
    gain2_grad = jnp.sum(grad_n2 * unit2, axis=0)
    grad_h1 = cotangent.astype(F32) + rms_norm_backward(grad_n2, unit2, inv2, gain2)
    grad_attn = grad_h1.astype(BF16)
    grad_heads = lax.dot_general(
        grad_attn.reshape(ntok, replicas, width // replicas),
        w_out_cols,
        (((1, 2), (0, 2)), ((), ())),
        preferred_element_type=F32,
    ).astype(BF16)
    grad_heads = line.exchange([grad_heads[:, k * qw : (k + 1) * qw] for k in range(groups)])
    down = [dot(after(part, grad_attn), w_down, ((1,), (0,))).astype(BF16) for part in hidden]
    grad_heads = jnp.concatenate(after(grad_heads, down))
    grad_qkv, own_qkv = attention_backward(
        hl, kvl, q_rot, k_rot, values, attended, lse, grad_heads, cosine, sine, start, place
    )
    qkv_grad = dot(normed1, grad_qkv, ((0,), (0,))).astype(BF16)
    grad_n1 = dot(own_qkv, w_qkv, ((1,), (1,))).astype(BF16)
    grad_n1 = line.scatter_sum(cut(grad_n1))
    n1_hops = line.hops
    grad_attn_all = line.gather(grad_attn, (grad_heads, own_qkv, n1_hops[0]))
    inv1 = inverse_rms(x_own)
    unit1 = x_own * inv1
    gain1_grad = jnp.sum(grad_n1 * unit1, axis=0)
    x_grad = (grad_h1 + rms_norm_backward(grad_n1, unit1, inv1, gain1)).astype(BF16)
    down = after(down, grad_attn_all[-1])
    down = line.scatter_sum(cut(down[0])[:half] + cut(down[1])[:half])
    mixed = (h1 + down).astype(BF16)

    grad_attn_all = jnp.concatenate(after(grad_attn_all, grad_n1))
    out_grad = dot(attended_low, grad_attn_all, ((0,), (0,))).astype(BF16)
    gain_grads = jnp.stack([gain1_grad, gain2_grad]).reshape(2, groups, replicas, rows)
    gain_grads = gain_grads.transpose(2, 3, 1, 0).astype(BF16)
    gain_grads = jnp.pad(gain_grads, ((0, 0), (0, 0), (0, 0), (0, 128 - 2)))
    qkv_grad = qkv_grad.reshape(groups, replicas, rows, qkvw).transpose(1, 2, 0, 3)
    wide = groups * (qkvw + 128)
    grads = jnp.concatenate([qkv_grad, gain_grads], axis=3).reshape(replicas, rows, wide)
    grads = jnp.concatenate([grads, out_grad.reshape(replicas, rows, width)], axis=2)

    def by_group(value):
        return line.exchange([line.at(value, k) for k in range(groups)])

    gu_grad, down_grad = after((gu_grad, down_grad), n1_hops[-2])
    gu_grad = line.ordered(by_group(gu_grad))
    down_grad = over_plane(down_grad).reshape(ffs, width)
    gu_grad = jnp.concatenate([part.reshape(rows, 2, ffs) for part in gu_grad], axis=2)
    gu_grad = over_plane(after(gu_grad, down_grad))
    grads = sum_plane(after(grads, gu_grad))

    out_grad = grads[:, wide:]
    grads = jnp.swapaxes(grads[:, :wide].reshape(rows, groups, qkvw + 128), 0, 1)
    grads = by_group(grads)
    gain_grads = sum([part[:, qkvw:].astype(F32) for part in grads]).astype(BF16)
    grads = line.ordered(grads)
    grads = [part[:, :qw] for part in grads] + [
        part[:, qw + j * kw : qw + (j + 1) * kw] for j in range(2) for part in grads
    ]
    grads = over_plane(after(jnp.concatenate(grads + [out_grad, gain_grads], axis=1), mixed))
    gu_grad = gu_grad.reshape(shard, 2, ff).astype(F32)
    down_grad = down_grad.astype(F32)
    grads = grads.reshape(shard, -1).astype(F32)
    q_grad = grads[:, :width]
    kv_grad = grads[:, width : width + 2 * groups * kw].reshape(shard, 2, groups * kw)
    out_grad = grads[:, width + 2 * groups * kw : 2 * width + 2 * groups * kw]
    gain_grads = grads[:, -128:]
    return (
        mixed,
        x_grad,
        gain_grads[:, 0],
        q_grad,
        kv_grad,
        out_grad,
        gain_grads[:, 1],
        gu_grad,
        down_grad,
    )


def solution(mesh):
    rows = P(("replica", "group"), None)
    flat, two, three = P("group"), P("group", None), P("group", None, None)
    return jax.shard_map(
        local,
        mesh=mesh,
        in_specs=(
            rows,
            rows,
            P("replica", None),
            P("replica", None),
            flat,
            two,
            three,
            two,
            flat,
            three,
            two,
        ),
        out_specs=(rows, rows, flat, two, three, two, flat, three, two),
        check_vma=False,
    )
```

```python
import functools
import math

import jax
import jax.numpy as jnp
from jax import lax
from jax.experimental import pallas as pl
from jax.experimental.pallas import tpu as pltpu
from jax.sharding import PartitionSpec as P

HEADS = 32
KV_HEADS = 8
HEAD_DIM = 64
EPS = 1e-05
NEG = -1e30
F32 = jnp.float32
BF16 = jnp.bfloat16
LIGHT = pl.CostEstimate(flops=1, bytes_accessed=1, transcendentals=0)
HEAVY = pl.CostEstimate(flops=3 * 10**11, bytes_accessed=1, transcendentals=0)


def frequencies(head_size):
    half = head_size // 2
    expo = jnp.arange(half).astype(F32) * (2.0 / head_size)
    base = jnp.power(F32(500000.0), -expo)
    wavelen = 2.0 * math.pi / base
    smooth = (8192.0 / wavelen - 1.0) / 3.0
    middle = (1.0 - smooth) * base / 32.0 + smooth * base
    return jnp.where(wavelen < 2048.0, base, jnp.where(wavelen > 8192.0, base / 32.0, middle))


def stream_meta(lengths_row, stream):
    ends = jnp.cumsum(lengths_row)
    past = ends[None, :] <= stream[:, None]
    segment = jnp.sum(past.astype(jnp.int32), axis=1)
    before = jnp.sum(jnp.where(past, lengths_row[None, :], 0), axis=1)
    return (segment, stream - before)


def inverse_rms(value):
    return lax.rsqrt(jnp.mean(value * value, axis=-1, keepdims=True) + EPS)


def rms_norm_backward(grad, unit, inverse, gain):
    scaled = grad * gain
    return inverse * (scaled - unit * jnp.mean(scaled * unit, axis=-1, keepdims=True))


def swap_halves(value):
    wide = value.shape[-1]
    lane = lax.broadcasted_iota(jnp.int32, value.shape, 1)
    low = lane % HEAD_DIM < HEAD_DIM // 2
    return jnp.where(
        low,
        pltpu.roll(value, wide - HEAD_DIM // 2, 1),
        pltpu.roll(value, HEAD_DIM // 2, 1),
    )


def rotate(value, cosine, sine, width):
    copies = value.shape[-1] // cosine.shape[-1]
    cosine = jnp.concatenate([cosine] * copies, axis=1)
    sine = jnp.concatenate([sine] * copies, axis=1)
    lane = lax.broadcasted_iota(jnp.int32, value.shape, 1)
    return jnp.where(lane < width, value * cosine + swap_halves(value) * sine, value)


def dot(left, right, dims):
    return lax.dot_general(left, right, (dims, ((), ())), preferred_element_type=F32)


def stacked(ref, rows, first, share):
    return jnp.concatenate(
        [ref[rows, (first + h) * HEAD_DIM : (first + h + 1) * HEAD_DIM] for h in range(share)], axis=0
    )


def bias_of(start, row0, block, keys):
    row = row0 + lax.broadcasted_iota(jnp.int32, (block, keys), 0)
    col = lax.broadcasted_iota(jnp.int32, (block, keys), 1)
    return jnp.where((col <= row) & (col >= start), 0.0, NEG).astype(F32)


def forward_kernel(
    hl, kvl, block, qkv_ref, cos_ref, sin_ref, start_ref, place_ref,
    q_ref, k_ref, v_ref, att_ref, lse_ref, low_ref,
):
    total = qkv_ref.shape[0]
    share = hl // kvl
    qw, kw = hl * HEAD_DIM, kvl * HEAD_DIM
    for row0 in range(0, total, block):
        rows = pl.ds(row0, block)
        turned = rotate(qkv_ref[rows, :], cos_ref[rows, :], sin_ref[rows, :], qw + kw)
        q_ref[rows, :] = (turned[:, :qw].astype(BF16) * HEAD_DIM ** (-0.5)).astype(BF16)
        k_ref[rows, :] = turned[:, qw : qw + kw].astype(BF16)
        v_ref[rows, :] = turned[:, qw + kw :].astype(BF16)
    for row0 in range(0, total, block):
        rows = pl.ds(row0, block)
        keys = row0 + block
        bias = bias_of(start_ref[rows, :], row0, block, keys)
        for kv in range(kvl):
            cols = slice(kv * HEAD_DIM, (kv + 1) * HEAD_DIM)
            query = stacked(q_ref, rows, kv * share, share)
            raw = dot(query, k_ref[:keys, cols], ((1,), (1,)))
            raw = (raw.reshape(share, block, keys) + bias[None]).reshape(share * block, keys)
            top = jnp.max(raw, axis=-1, keepdims=True)
            probs = jnp.exp(raw - top)
            total_p = jnp.sum(probs, axis=-1, keepdims=True)
            out = dot(probs.astype(BF16), v_ref[:keys, cols], ((1,), (0,))) / total_p
            lse = top + jnp.log(total_p)
            for h in range(share):
                head = kv * share + h
                part = slice(h * block, (h + 1) * block)
                att_ref[rows, head * HEAD_DIM : (head + 1) * HEAD_DIM] = out[part]
                lse_ref[rows, head : head + 1] = lse[part]
    low_ref[...] = dot(place_ref[...], att_ref[...].astype(BF16), ((0,), (0,))).astype(BF16)


def backward_kernel(
    hl, kvl, block, q_ref, k_ref, v_ref, att_ref, lse_ref, heads_ref, cos_ref, sin_ref, start_ref, place_ref,
    grad_ref, native_ref, gh_ref, gq_ref, gk_ref, gv_ref,
):
    total = q_ref.shape[0]
    share = hl // kvl
    qw, kw = hl * HEAD_DIM, kvl * HEAD_DIM
    gh_ref[...] = dot(place_ref[...], heads_ref[...], ((1,), (0,))).astype(BF16)
    gk_ref[...] = jnp.zeros_like(gk_ref)
    gv_ref[...] = jnp.zeros_like(gv_ref)
    for row0 in range(0, total, block):
        rows = pl.ds(row0, block)
        keys = row0 + block
        bias = bias_of(start_ref[rows, :], row0, block, keys)
        for kv in range(kvl):
            cols = slice(kv * HEAD_DIM, (kv + 1) * HEAD_DIM)
            query = stacked(q_ref, rows, kv * share, share)
            heads = stacked(gh_ref, rows, kv * share, share)
            att = stacked(att_ref, rows, kv * share, share)
            delta = jnp.sum(heads.astype(F32) * att, axis=-1, keepdims=True)
            lse = jnp.concatenate(
                [lse_ref[rows, kv * share + h : kv * share + h + 1] for h in range(share)], axis=0
            )
            raw = dot(query, k_ref[:keys, cols], ((1,), (1,)))
            raw = (raw.reshape(share, block, keys) + bias[None]).reshape(share * block, keys)
            probs = jnp.exp(raw - lse)
            grad_probs = dot(heads, v_ref[:keys, cols], ((1,), (1,)))
            scores = (probs * (grad_probs - delta)).astype(BF16)
            out = dot(scores, k_ref[:keys, cols], ((1,), (0,))) * HEAD_DIM ** (-0.5)
            for h in range(share):
                head = kv * share + h
                gq_ref[rows, head * HEAD_DIM : (head + 1) * HEAD_DIM] = out[h * block : (h + 1) * block]
            gk_ref[:keys, cols] += dot(scores, query, ((0,), (0,)))
            gv_ref[:keys, cols] += dot(probs.astype(BF16), heads, ((0,), (0,)))
    for row0 in range(0, total, block):
        rows = pl.ds(row0, block)
        grad = jnp.concatenate([gq_ref[rows, :], gk_ref[rows, :], gv_ref[rows, :]], axis=1)
        grad_ref[rows, :] = rotate(grad, cos_ref[rows, :], -sin_ref[rows, :], qw + kw).astype(BF16)
    native_ref[...] = dot(place_ref[...], grad_ref[...], ((0,), (0,))).astype(BF16)


def vmem(count):
    return [pl.BlockSpec(memory_space=pltpu.VMEM)] * count


def attention_forward(hl, kvl, qkv, cosine, sine, start, place):
    total = qkv.shape[0]
    block = 256 if total <= 1024 else 128
    qw, kw = hl * HEAD_DIM, kvl * HEAD_DIM
    shape = jax.ShapeDtypeStruct
    return pl.pallas_call(
        functools.partial(forward_kernel, hl, kvl, block),
        out_shape=(
            shape((total, qw), BF16), shape((total, kw), BF16), shape((total, kw), BF16),
            shape((total, qw), F32), shape((total, 128), F32), shape((total, qw), BF16),
        ),
        in_specs=vmem(5), out_specs=tuple(vmem(6)),
        compiler_params=pltpu.CompilerParams(vmem_limit_bytes=56 * 2**20),
        cost_estimate=LIGHT,
        name="attention_forward",
    )(qkv, cosine, sine, start, place)


def attention_backward(hl, kvl, q, k, v, att, lse, heads, cosine, sine, start, place):
    total = q.shape[0]
    block = 256 if total <= 1024 else 128
    qw, kw = hl * HEAD_DIM, kvl * HEAD_DIM
    shape = jax.ShapeDtypeStruct
    return pl.pallas_call(
        functools.partial(backward_kernel, hl, kvl, block),
        out_shape=(shape((total, qw + 2 * kw), BF16), shape((total, qw + 2 * kw), BF16)),
        in_specs=vmem(10), out_specs=tuple(vmem(2)),
        scratch_shapes=[
            pltpu.VMEM((total, qw), BF16), pltpu.VMEM((total, qw), F32),
            pltpu.VMEM((total, kw), F32), pltpu.VMEM((total, kw), F32),
        ],
        compiler_params=pltpu.CompilerParams(vmem_limit_bytes=56 * 2**20),
        cost_estimate=pl.CostEstimate(flops=4 * 10**10, bytes_accessed=1, transcendentals=0),
        name="attention_backward",
    )(q, k, v, att, lse, heads, cosine, sine, start, place)


def hidden_kernel(
    parts, n2_ref, dy_ref, up_ref, down_ref, hidden_ref, gate_grad_ref, up_grad_ref, grad_ref, grad_sum
):
    step = pl.program_id(0)
    wide = down_ref.shape[0] // parts
    total = None
    for part in range(parts):
        cols = slice(part * wide, (part + 1) * wide)
        both = dot(n2_ref[...], up_ref[part], ((1,), (0,)))
        gate, up = both[:, :wide], both[:, wide:]
        grad = dot(dy_ref[...], down_ref[cols, :], ((1,), (1,)))
        sigma = 1.0 / (1.0 + jnp.exp(-gate))
        silu = gate * sigma
        hidden_ref[:, cols] = (silu * up).astype(BF16)
        grad_gate = (grad * up * sigma * (1.0 + gate * (1.0 - sigma))).astype(BF16)
        grad_up = (grad * silu).astype(BF16)
        gate_grad_ref[:, cols] = grad_gate
        up_grad_ref[:, cols] = grad_up
        both = jnp.concatenate([grad_gate, grad_up], axis=1)
        both = dot(both, up_ref[part], ((1,), (1,)))
        total = both if total is None else total + both

    @pl.when(step == 0)
    def _():
        grad_sum[...] = total

    @pl.when(step > 0)
    def _():
        grad_sum[...] += total

    @pl.when(step == pl.num_programs(0) - 1)
    def _():
        grad_ref[...] = grad_sum[...].astype(BF16)


def feed_forward(n2, dy, w_gu, w_down, cost):
    rows, width = n2.shape
    ffs = w_down.shape[0]
    count, _, both = w_gu.shape
    wide = both // 2
    parts = max(1, 512 // wide)
    tile = parts * wide
    shape = jax.ShapeDtypeStruct
    whole = pl.BlockSpec((rows, width), lambda j: (0, 0), pipeline_mode=pl.Buffered(1))
    return pl.pallas_call(
        functools.partial(hidden_kernel, parts),
        grid=(count // parts,),
        in_specs=[
            whole,
            whole,
            pl.BlockSpec((parts, width, both), lambda j: (j, 0, 0)),
            pl.BlockSpec((tile, width), lambda j: (j, 0)),
        ],
        out_specs=[pl.BlockSpec((rows, tile), lambda j: (0, j))] * 3 + [whole],
        out_shape=[shape((rows, ffs), BF16)] * 3 + [shape((rows, width), BF16)],
        scratch_shapes=[pltpu.VMEM((rows, width), F32)],
        compiler_params=pltpu.CompilerParams(vmem_limit_bytes=60 * 2**20),
        cost_estimate=cost,
        name="feed_forward",
    )(n2, dy, w_gu, w_down)


def product_kernel(parts, *refs):
    lefts, rights = refs[:parts], refs[parts:-3]
    out_ref, done_ref, turned_ref = refs[-3:]
    count = len(rights) // parts
    step = pl.program_id(1)
    each = pl.num_programs(1) // count
    size = lefts[0].shape[0]

    @pl.when(step == 0)
    def _():
        for part in range(parts):
            turned_ref[:, part * size : (part + 1) * size] = lefts[part][...].T
        done_ref[...] = jnp.zeros_like(done_ref)

    for which in range(count):

        @pl.when((step >= which * each) & (step < (which + 1) * each))
        def _():
            value = 0.0
            for part in range(parts):
                turned = turned_ref[:, part * size : (part + 1) * size]
                value += dot(turned, rights[which * parts + part][...], ((1,), (0,)))
            out_ref[...] = value.astype(BF16).reshape(out_ref.shape)


def weight_gradient(lefts, rights, blocks, replicas, by_block):
    parts, (size, width) = len(lefts), lefts[0].shape
    cols = rights[0][0].shape[1]
    rows = width // blocks
    tile = min(1024, cols)
    each = cols // tile

    def place(which):
        return lambda i, j: (0, jnp.clip(j - which * each, 0, each - 1))

    if by_block:
        shape = (replicas, blocks, rows // replicas, len(rights) * cols)
        out_spec = pl.BlockSpec((replicas, 1, rows // replicas, tile), lambda i, j: (0, i, 0, j))
    else:
        shape = (width, len(rights) * cols)
        out_spec = pl.BlockSpec((rows, tile), lambda i, j: (i, j))
    return pl.pallas_call(
        functools.partial(product_kernel, parts),
        grid=(blocks, len(rights) * each),
        in_specs=[pl.BlockSpec((size, rows), lambda i, j: (0, i))] * parts
        + [pl.BlockSpec((size, tile), place(n)) for n in range(len(rights)) for _ in range(parts)],
        out_specs=[out_spec, pl.BlockSpec((8, 128), lambda i, j: (0, 0))],
        out_shape=[jax.ShapeDtypeStruct(shape, BF16), jax.ShapeDtypeStruct((8, 128), F32)],
        scratch_shapes=[pltpu.VMEM((rows, parts * size), BF16)],
        compiler_params=pltpu.CompilerParams(vmem_limit_bytes=56 * 2**20),
        cost_estimate=LIGHT,
        name="weight_gradient",
    )(*lefts, *[part for right in rights for part in right])


def mark(value):
    while value.ndim > 2:
        value = value[0]
    return value[:8, :128]


def after(value, *others, cost=LIGHT):
    leaves, tree = jax.tree.flatten(value)
    others = [mark(other) for other in jax.tree.leaves(others)]
    anywhere = pl.BlockSpec(memory_space=pl.ANY)
    tied = pl.pallas_call(
        lambda *refs: None,
        out_shape=[jax.ShapeDtypeStruct(leaf.shape, leaf.dtype) for leaf in leaves],
        in_specs=[anywhere] * (len(leaves) + len(others)),
        out_specs=[anywhere] * len(leaves),
        input_output_aliases={i: i for i in range(len(leaves))},
        cost_estimate=cost,
        name="after",
    )(*leaves, *others)
    return jax.tree.unflatten(tree, tied)


def pair_kernel(odd_ref, own_ref, low_ref, high_ref, out_ref):
    size = own_ref.shape[0]
    out_ref[:size, :] = own_ref[...]

    @pl.when(odd_ref[0] == 0)
    def _():
        out_ref[size:, :] = high_ref[...]

    @pl.when(odd_ref[0] != 0)
    def _():
        out_ref[size:, :] = low_ref[...]


class Line:
    def __init__(self, count):
        self.count = count
        self.me = lax.axis_index("group")

    def swap(self, value, slot):
        return lax.ppermute(value, "group", [(i, i ^ slot) for i in range(self.count)])

    def at(self, value, slot, axis=0):
        return lax.dynamic_index_in_dim(value, self.me ^ slot, axis, keepdims=False)

    def exchange(self, slots):
        return [slots[0]] + [self.swap(slots[k], k) for k in range(1, self.count)]

    def ordered(self, slots):
        return [self.pick(slots, j) for j in range(self.count)]

    def pick(self, slots, device):
        value = slots[0]
        for k in range(1, self.count):
            value = jnp.where(self.me == device ^ k, slots[k], value)
        return value

    def near(self, begun):
        (own, low), (_, high) = begun
        size, cols = own.shape
        return pl.pallas_call(
            pair_kernel,
            out_shape=jax.ShapeDtypeStruct((2 * size, cols), own.dtype),
            in_specs=[pl.BlockSpec(memory_space=pltpu.SMEM)] + vmem(3),
            out_specs=pl.BlockSpec(memory_space=pltpu.VMEM),
            compiler_params=pltpu.CompilerParams(vmem_limit_bytes=16 * 2**20),
            cost_estimate=LIGHT,
            name="pair",
        )(self.me.reshape(1) % 2, own, low, high)

    def gather(self, value, gates=(), hops=None, begun=None):
        count = self.count
        low, high = begun if begun else ([value], [value])
        low, high = list(low), list(high)
        for hop in range(len(low), (hops or count - 1) + 1):
            moving = (low[-1], high[-1])
            if hop <= len(gates) and gates[hop - 1] is not None:
                if hop == 1:
                    moving = (after(value, gates[0]),) * 2
                else:
                    moving = low[-1], high[-1] = after(moving, gates[hop - 1])
            up = [(i, i + 1) for i in range(hop - 1, count - 1)]
            down = [(i + 1, i) for i in range(count - hop)]
            low.append(lax.ppermute(moving[0], "group", up))
            high.append(lax.ppermute(moving[1], "group", down))
        if hops:
            return low, high
        self.last = (low[1:], high[1:])
        slots = [value]
        for k in range(1, count):
            chosen = None
            for device in range(count):
                source = device ^ k
                came = high[source - device] if source > device else low[device - source]
                chosen = came if chosen is None else jnp.where(self.me == device, came, chosen)
            slots.append(chosen)
        return slots

    def scatter_hop(self, slots, came, hop, gate=()):
        count = self.count
        up = [(i, i + 1) for i in range(count - hop)]
        down = [(i + 1, i) for i in range(hop - 1, count - 1)]
        moving = [self.pick_far(slots, hop), self.pick_far(slots, -hop)]
        if came:
            moving = [mine + part for mine, part in zip(moving, came)]
        if gate:
            moving = after(moving, gate)
        return (lax.ppermute(moving[0], "group", up), lax.ppermute(moving[1], "group", down))

    def scatter_sum(self, slots):
        came = None
        for hop in range(self.count - 1, 0, -1):
            came = self.scatter_hop(slots, came, hop)
        return slots[0].astype(F32) + came[0].astype(F32) + came[1].astype(F32)

    def pick_far(self, slots, distance):
        chosen = slots[1]
        for device in range(self.count):
            other = device + distance
            if 0 <= other < self.count:
                chosen = jnp.where(self.me == device, slots[device ^ other], chosen)
        return chosen


def gather_plane(value, replicas, me):
    bits = [1 << i for i in range(1, replicas.bit_length() - 1)]
    middle = value.shape[0] // 2

    def swap(part, bit):
        return lax.ppermute(part, "replica", [(i, i ^ bit) for i in range(replicas)])

    halves = []
    for half, order in ((value[:middle], bits), (value[middle:], bits[::-1])):
        held, places = half[None], [0]
        for bit in order:
            held = jnp.concatenate([held, swap(held, bit)])
            places = places + [place ^ bit for place in places]
        halves.append(jnp.stack([held[places.index(2 * i)] for i in range(replicas // 2)]))
    held = jnp.concatenate(halves, axis=1)
    held = jnp.stack([held, swap(held, 1)], axis=1)
    held = held.reshape(replicas, *value.shape)
    return jnp.stack(
        [lax.dynamic_index_in_dim(held, me ^ i, 0, keepdims=False) for i in range(replicas)]
    )


def local(
    tokens,
    cotangent,
    lengths,
    packing,
    attn_gain,
    w_query,
    w_key_value,
    w_out,
    mlp_gain,
    w_gate_up,
    w_down,
):
    ntok, width = tokens.shape
    total = packing.shape[1]
    groups = total // ntok
    shard = w_query.shape[0]
    replicas = lax.axis_size("replica")
    rows = shard // replicas
    kvl = KV_HEADS // groups
    hl = HEADS // groups
    qw = hl * HEAD_DIM
    kw = kvl * HEAD_DIM
    qkvw = qw + 2 * kw
    ff = w_gate_up.shape[2]
    ffs = ff // groups
    me_r = lax.axis_index("replica")
    line = Line(groups)

    def own_rows(value):
        return lax.dynamic_slice_in_dim(value, me_r * rows, rows)

    def over_plane(value):
        return lax.all_gather(value, "replica", axis=0)

    wq_rows = own_rows(w_query).reshape(rows, groups, qw)
    wkv_rows = own_rows(w_key_value).reshape(rows, 2, groups, kw)
    wkv_rows = wkv_rows.transpose(0, 2, 1, 3).reshape(rows, groups, 2 * kw)
    qkv_rows = jnp.concatenate([wq_rows, wkv_rows], axis=2)
    ffr = ffs // replicas
    gu_cols = []
    for k in range(groups):
        first = (line.me ^ k) * ffs + me_r * ffr
        part = lax.dynamic_slice(w_gate_up, (0, 0, first), (shard, 2, ffr))
        gu_cols.append(jnp.concatenate([part[:, 0], part[:, 1]], axis=1))
    gu_cols = jnp.stack(gu_cols)
    out_cols = lax.dynamic_slice_in_dim(w_out, me_r * (width // replicas), width // replicas, 1)

    w_qkv = line.exchange([line.at(qkv_rows, k, 1) for k in range(groups)])
    gains = jnp.stack([attn_gain, mlp_gain])
    gains = jnp.concatenate(line.ordered(line.exchange([gains] * groups)), axis=1)
    gain1, gain2 = gains[0], gains[1]
    w_out_cols = line.exchange([out_cols] * groups)
    x_hops = line.gather(tokens, (), 1)
    x_came = [part[1] for part in x_hops]
    w_qkv, w_out_cols[1:], x_came = after((w_qkv, w_out_cols[1:], x_came), gu_cols)
    x_hops = [[tokens, part] for part in x_came]
    seats = jnp.arange(total, dtype=jnp.int32)
    _, position = stream_meta(lengths[0], seats)
    start = (seats - position)[:, None]
    angles = position.astype(F32)[:, None] * frequencies(HEAD_DIM)[None, :]
    copies = 128 // HEAD_DIM
    cosine = jnp.tile(jnp.cos(angles), (1, 2 * copies))
    sine = jnp.sin(angles)
    sine = jnp.tile(jnp.concatenate([-sine, sine], axis=1), (1, copies))
    seat = packing.reshape(groups, ntok)
    seat = jnp.concatenate([line.at(seat, k) for k in range(groups)])
    place = (seat[None, :] == seats[:, None]).astype(BF16)
    w_qkv = over_plane(jnp.stack(line.ordered(w_qkv)))
    w_qkv = jnp.swapaxes(w_qkv, 0, 1).reshape(width, qkvw)
    x_slots = line.gather(tokens, (), 0, x_hops)
    x_last = [part[-1] for part in line.last]
    w_out_cols = over_plane(jnp.concatenate(w_out_cols))
    gu_cols = after(gu_cols, x_last)
    gu_cols = line.exchange([gu_cols[k] for k in range(groups)])
    dy_hops = line.gather(cotangent, (x_last,), 1)

    def normed(value):
        value = value.astype(F32)
        return (value * inverse_rms(value) * gain1).astype(BF16)

    normed1 = jnp.concatenate([normed(value) for value in x_slots])
    normed1 = dot(place, normed1, ((1,), (0,))).astype(BF16)
    qkv = dot(normed1, w_qkv, ((1,), (0,)))
    q_rot, k_rot, values, attended, lse, attended_low = attention_forward(
        hl, kvl, qkv, cosine, sine, start, place
    )

    def cut(value):
        return [value[k * ntok : (k + 1) * ntok] for k in range(groups)]

    dy_near = dy_hops
    attended_low = after(attended_low, [part[1] for part in dy_hops])
    own_attended = line.exchange(cut(attended_low))
    w_gu = over_plane(jnp.concatenate(line.ordered(after(gu_cols, attended_low))))
    x_own = tokens.astype(F32)
    own_attended_all = jnp.concatenate(own_attended, axis=1)
    h1 = lax.dot_general(own_attended_all, w_out_cols, (((1,), (1,)), ((), ())), preferred_element_type=F32)
    h1 = x_own + h1.reshape(ntok, width)
    inv2 = inverse_rms(h1)
    unit2 = h1 * inv2
    normed2 = (unit2 * gain2).astype(BF16)
    n2_near = line.gather(normed2, (), 1)
    dy_hops = line.gather(cotangent, (None, own_attended[1:]), 2, dy_hops)
    near_parts = [line.near(n2_near), line.near(dy_near)]

    half = groups // 2
    if half > 2:
        n2, dy = line.gather(normed2, (), 0, n2_near), line.gather(cotangent, (), 0, dy_hops)
        near_parts = [jnp.concatenate(part[:half]) for part in (n2, dy)]
    near = feed_forward(*near_parts, w_gu, w_down, HEAVY)
    if half == 2:
        n2 = line.gather(normed2, (None, None, near[3]), 0, n2_near)
        dy_hops = line.gather(cotangent, (None, None, n2_near), 3, dy_hops)
        for part, last in zip(dy_hops, after([part[-1] for part in dy_hops], near[3])):
            part[-1] = last
        dy = line.gather(cotangent, (), 0, dy_hops)
    n2_parts = [near_parts[0], jnp.concatenate(n2[half:])]
    dy_parts = [near_parts[1], jnp.concatenate(dy[half:])]
    n2_parts[1] = after(n2_parts[1], near[3])
    far = feed_forward(n2_parts[1], dy_parts[1], w_gu, w_down, LIGHT)
    grad_n2 = line.exchange(cut(near[3])[:half] + cut(far[3])[:half])

    def sum_plane(value):
        return lax.psum_scatter(value, "replica", scatter_dimension=0)

    hidden = [near[0], far[0]]
    down_grad, down_done = weight_gradient(hidden, [dy_parts], groups, replicas, False)
    n2_parts[0] = after(n2_parts[0], down_done)
    gu_grad, gu_done = weight_gradient(
        n2_parts, [[near[1], far[1]], [near[2], far[2]]], groups, replicas, True
    )
    down_grad = sum_plane(down_grad.reshape(replicas, ffs // replicas, width))
    gu_grad = gu_grad.reshape(replicas, groups * rows, 2 * ffs)
    gu_grad = sum_plane(gu_grad).reshape(groups, rows, 2 * ffs)

    grad_n2 = after(grad_n2, gu_done, cost=HEAVY)
    grad_n2 = sum([part.astype(F32) for part in grad_n2])
    gain2_grad = jnp.sum(grad_n2 * unit2, axis=0)
    grad_h1 = cotangent.astype(F32) + rms_norm_backward(grad_n2, unit2, inv2, gain2)
    grad_attn = grad_h1.astype(BF16)
    grad_heads = lax.dot_general(
        grad_attn.reshape(ntok, replicas, width // replicas),
        w_out_cols,
        (((1, 2), (0, 2)), ((), ())),
        preferred_element_type=F32,
    ).astype(BF16)
    heads_there = grad_heads
    grad_heads = line.exchange([grad_heads[:, k * qw : (k + 1) * qw] for k in range(groups)])
    grad_heads = jnp.concatenate(grad_heads)
    ga_hops = line.gather(grad_attn, (grad_heads,), 1)
    grad_qkv, own_qkv = attention_backward(
        hl, kvl, q_rot, k_rot, values, attended, lse, grad_heads, cosine, sine, start, place
    )
    down = [dot(after(part, own_qkv), w_down, ((1,), (0,))).astype(BF16) for part in hidden]
    down = cut(down[0])[:half] + cut(down[1])[:half]
    own_qkv = after(own_qkv, [part[1] for part in ga_hops])
    qkv_grad = dot(normed1, grad_qkv, ((0,), (0,))).astype(BF16)
    grad_n1 = dot(own_qkv, w_qkv, ((1,), (1,))).astype(BF16)

    def by_group(value):
        return line.exchange([line.at(value, k) for k in range(groups)])

    qkv_grad = qkv_grad.reshape(groups, replicas, rows, qkvw).transpose(1, 2, 0, 3)
    qkv_grad = qkv_grad.reshape(replicas, rows, groups * qkvw)
    n1_slots, n1_hops = cut(grad_n1), []
    for i in range(groups - 1):
        came = n1_hops[-1] if n1_hops else None
        gate = [part[-1] for part in ga_hops] if i else ()
        n1_hops.append(line.scatter_hop(n1_slots, came, groups - 1 - i, gate))
        if i + 2 < groups:
            gates = [None] * (i + 1) + [came if i else own_qkv]
            ga_hops = line.gather(grad_attn, gates, i + 2, ga_hops)
    gu_grad, down_grad, qkv_grad = after((gu_grad, down_grad, qkv_grad), n1_hops[0])
    qkv_grad = sum_plane(qkv_grad)
    down_grad = over_plane(down_grad).reshape(ffs, width)
    gu_grad = by_group(after(gu_grad, n1_hops[-2]))
    grad_n1 = sum(part.astype(F32) for part in (n1_slots[0], *n1_hops[-1]))
    grad_attn_all = line.gather(grad_attn, (), 0, ga_hops)
    inv1 = inverse_rms(x_own)
    unit1 = x_own * inv1
    gain1_grad = jnp.sum(grad_n1 * unit1, axis=0)
    x_grad = (grad_h1 + rms_norm_backward(grad_n1, unit1, inv1, gain1)).astype(BF16)

    grad_attn_all = jnp.concatenate(after(grad_attn_all, grad_n1))
    out_grad = dot(attended_low, grad_attn_all, ((0,), (0,))).astype(BF16)
    gain_grads = jnp.stack([gain1_grad, gain2_grad]).reshape(2, groups, replicas, rows)
    gain_grads = gain_grads.transpose(2, 3, 1, 0).astype(BF16)
    gain_grads = jnp.pad(gain_grads, ((0, 0), (0, 0), (0, 0), (0, 128 - 2)))
    out_grad = out_grad.reshape(replicas, rows, width)
    gain_grads = gain_grads.reshape(replicas, rows, groups * 128)
    out_grad = jnp.concatenate([out_grad, gain_grads], axis=2)
    out_grad = sum_plane(after(out_grad, down_grad, qkv_grad))
    y_hops = []
    for hop in range(groups - 1, 0, -1):
        gate = () if y_hops else n1_hops[-1]
        y_hops.append(line.scatter_hop(down, y_hops[-1] if y_hops else None, hop, gate))
    mixed = (h1 + sum(part.astype(F32) for part in (down[0], *y_hops[-1]))).astype(BF16)

    gu_grad = line.ordered(gu_grad)
    gu_grad = jnp.concatenate([part.reshape(rows, 2, ffs) for part in gu_grad], axis=2)
    gu_grad = over_plane(after(gu_grad, out_grad, y_hops[-2]))

    grads = jnp.concatenate(
        [qkv_grad.reshape(rows, groups, qkvw), out_grad[:, width:].reshape(rows, groups, 128)], axis=2
    )
    grads = by_group(jnp.swapaxes(grads, 0, 1))
    gain_grads = sum([part[:, qkvw:].astype(F32) for part in grads]).astype(BF16)
    grads = line.ordered(grads)
    grads = [part[:, :qw] for part in grads] + [
        part[:, qw + j * kw : qw + (j + 1) * kw] for j in range(2) for part in grads
    ]
    grads = jnp.concatenate(grads + [out_grad[:, :width], gain_grads], axis=1)
    grads = gather_plane(grads, replicas, me_r)
    gu_grad = gu_grad.reshape(shard, 2, ff).astype(F32)
    down_grad = down_grad.astype(F32)
    grads = grads.reshape(shard, -1).astype(F32)
    q_grad = grads[:, :width]
    kv_grad = grads[:, width : width + 2 * groups * kw].reshape(shard, 2, groups * kw)
    out_grad = grads[:, width + 2 * groups * kw : 2 * width + 2 * groups * kw]
    gain_grads = grads[:, -128:]
    return (
        mixed,
        x_grad,
        gain_grads[:, 0],
        q_grad,
        kv_grad,
        out_grad,
        gain_grads[:, 1],
        gu_grad,
        down_grad,
    )


def solution(mesh):
    rows = P(("replica", "group"), None)
    flat, two, three = P("group"), P("group", None), P("group", None, None)
    return jax.shard_map(
        local,
        mesh=mesh,
        in_specs=(
            rows,
            rows,
            P("replica", None),
            P("replica", None),
            flat,
            two,
            three,
            two,
            flat,
            three,
            two,
        ),
        out_specs=(rows, rows, flat, two, three, two, flat, three, two),
        check_vma=False,
    )
```

```python
import functools
import math

import jax
import jax.numpy as jnp
from jax import lax
from jax.experimental import pallas as pl
from jax.experimental.pallas import tpu as pltpu
from jax.sharding import PartitionSpec as P

HEADS = 32
KV_HEADS = 8
HEAD_DIM = 64
EPS = 1e-05
NEG = -1e30
F32 = jnp.float32
BF16 = jnp.bfloat16
LIGHT = pl.CostEstimate(flops=1, bytes_accessed=1, transcendentals=0)
HEAVY = pl.CostEstimate(flops=3 * 10**11, bytes_accessed=1, transcendentals=0)


def frequencies(head_size):
    half = head_size // 2
    expo = jnp.arange(half).astype(F32) * (2.0 / head_size)
    base = jnp.power(F32(500000.0), -expo)
    wavelen = 2.0 * math.pi / base
    smooth = (8192.0 / wavelen - 1.0) / 3.0
    middle = (1.0 - smooth) * base / 32.0 + smooth * base
    return jnp.where(wavelen < 2048.0, base, jnp.where(wavelen > 8192.0, base / 32.0, middle))


def stream_meta(lengths_row, stream):
    ends = jnp.cumsum(lengths_row)
    past = ends[None, :] <= stream[:, None]
    segment = jnp.sum(past.astype(jnp.int32), axis=1)
    before = jnp.sum(jnp.where(past, lengths_row[None, :], 0), axis=1)
    return (segment, stream - before)


def inverse_rms(value):
    return lax.rsqrt(jnp.mean(value * value, axis=-1, keepdims=True) + EPS)


def rms_norm_backward(grad, unit, inverse, gain):
    scaled = grad * gain
    return inverse * (scaled - unit * jnp.mean(scaled * unit, axis=-1, keepdims=True))


def swap_halves(value):
    wide = value.shape[-1]
    lane = lax.broadcasted_iota(jnp.int32, value.shape, 1)
    low = lane % HEAD_DIM < HEAD_DIM // 2
    return jnp.where(
        low,
        pltpu.roll(value, wide - HEAD_DIM // 2, 1),
        pltpu.roll(value, HEAD_DIM // 2, 1),
    )


def rotate(value, cosine, sine, width):
    copies = value.shape[-1] // cosine.shape[-1]
    cosine = jnp.concatenate([cosine] * copies, axis=1)
    sine = jnp.concatenate([sine] * copies, axis=1)
    lane = lax.broadcasted_iota(jnp.int32, value.shape, 1)
    return jnp.where(lane < width, value * cosine + swap_halves(value) * sine, value)


def dot(left, right, dims):
    return lax.dot_general(left, right, (dims, ((), ())), preferred_element_type=F32)


def stacked(ref, rows, first, share):
    return jnp.concatenate(
        [ref[rows, (first + h) * HEAD_DIM : (first + h + 1) * HEAD_DIM] for h in range(share)], axis=0
    )


def bias_of(start, row0, block, keys):
    row = row0 + lax.broadcasted_iota(jnp.int32, (block, keys), 0)
    col = lax.broadcasted_iota(jnp.int32, (block, keys), 1)
    return jnp.where((col <= row) & (col >= start), 0.0, NEG).astype(F32)


def forward_kernel(
    hl, kvl, block, qkv_ref, cos_ref, sin_ref, start_ref, place_ref,
    q_ref, k_ref, v_ref, att_ref, lse_ref, low_ref,
):
    total = qkv_ref.shape[0]
    share = hl // kvl
    qw, kw = hl * HEAD_DIM, kvl * HEAD_DIM
    for row0 in range(0, total, block):
        rows = pl.ds(row0, block)
        turned = rotate(qkv_ref[rows, :], cos_ref[rows, :], sin_ref[rows, :], qw + kw)
        q_ref[rows, :] = (turned[:, :qw].astype(BF16) * HEAD_DIM ** (-0.5)).astype(BF16)
        k_ref[rows, :] = turned[:, qw : qw + kw].astype(BF16)
        v_ref[rows, :] = turned[:, qw + kw :].astype(BF16)
    for row0 in range(0, total, block):
        rows = pl.ds(row0, block)
        keys = row0 + block
        bias = bias_of(start_ref[rows, :], row0, block, keys)
        for kv in range(kvl):
            cols = slice(kv * HEAD_DIM, (kv + 1) * HEAD_DIM)
            query = stacked(q_ref, rows, kv * share, share)
            raw = dot(query, k_ref[:keys, cols], ((1,), (1,)))
            raw = (raw.reshape(share, block, keys) + bias[None]).reshape(share * block, keys)
            top = jnp.max(raw, axis=-1, keepdims=True)
            probs = jnp.exp(raw - top)
            total_p = jnp.sum(probs, axis=-1, keepdims=True)
            out = dot(probs.astype(BF16), v_ref[:keys, cols], ((1,), (0,))) / total_p
            lse = top + jnp.log(total_p)
            for h in range(share):
                head = kv * share + h
                part = slice(h * block, (h + 1) * block)
                att_ref[rows, head * HEAD_DIM : (head + 1) * HEAD_DIM] = out[part]
                lse_ref[rows, head : head + 1] = lse[part]
    low_ref[...] = dot(place_ref[...], att_ref[...].astype(BF16), ((0,), (0,))).astype(BF16)


def backward_kernel(
    hl, kvl, block, q_ref, k_ref, v_ref, att_ref, lse_ref, heads_ref, cos_ref, sin_ref, start_ref, place_ref,
    grad_ref, native_ref, gh_ref, gq_ref, gk_ref, gv_ref,
):
    total = q_ref.shape[0]
    share = hl // kvl
    qw, kw = hl * HEAD_DIM, kvl * HEAD_DIM
    gh_ref[...] = dot(place_ref[...], heads_ref[...], ((1,), (0,))).astype(BF16)
    gk_ref[...] = jnp.zeros_like(gk_ref)
    gv_ref[...] = jnp.zeros_like(gv_ref)
    for row0 in range(0, total, block):
        rows = pl.ds(row0, block)
        keys = row0 + block
        bias = bias_of(start_ref[rows, :], row0, block, keys)
        for kv in range(kvl):
            cols = slice(kv * HEAD_DIM, (kv + 1) * HEAD_DIM)
            query = stacked(q_ref, rows, kv * share, share)
            heads = stacked(gh_ref, rows, kv * share, share)
            att = stacked(att_ref, rows, kv * share, share)
            delta = jnp.sum(heads.astype(F32) * att, axis=-1, keepdims=True)
            lse = jnp.concatenate(
                [lse_ref[rows, kv * share + h : kv * share + h + 1] for h in range(share)], axis=0
            )
            raw = dot(query, k_ref[:keys, cols], ((1,), (1,)))
            raw = (raw.reshape(share, block, keys) + bias[None]).reshape(share * block, keys)
            probs = jnp.exp(raw - lse)
            grad_probs = dot(heads, v_ref[:keys, cols], ((1,), (1,)))
            scores = (probs * (grad_probs - delta)).astype(BF16)
            out = dot(scores, k_ref[:keys, cols], ((1,), (0,))) * HEAD_DIM ** (-0.5)
            for h in range(share):
                head = kv * share + h
                gq_ref[rows, head * HEAD_DIM : (head + 1) * HEAD_DIM] = out[h * block : (h + 1) * block]
            gk_ref[:keys, cols] += dot(scores, query, ((0,), (0,)))
            gv_ref[:keys, cols] += dot(probs.astype(BF16), heads, ((0,), (0,)))
    for row0 in range(0, total, block):
        rows = pl.ds(row0, block)
        grad = jnp.concatenate([gq_ref[rows, :], gk_ref[rows, :], gv_ref[rows, :]], axis=1)
        grad_ref[rows, :] = rotate(grad, cos_ref[rows, :], -sin_ref[rows, :], qw + kw).astype(BF16)
    native_ref[...] = dot(place_ref[...], grad_ref[...], ((0,), (0,))).astype(BF16)


def vmem(count):
    return [pl.BlockSpec(memory_space=pltpu.VMEM)] * count


def attention_forward(hl, kvl, qkv, cosine, sine, start, place):
    total = qkv.shape[0]
    block = 256 if total <= 1024 else 128
    qw, kw = hl * HEAD_DIM, kvl * HEAD_DIM
    shape = jax.ShapeDtypeStruct
    return pl.pallas_call(
        functools.partial(forward_kernel, hl, kvl, block),
        out_shape=(
            shape((total, qw), BF16), shape((total, kw), BF16), shape((total, kw), BF16),
            shape((total, qw), F32), shape((total, 128), F32), shape((total, qw), BF16),
        ),
        in_specs=vmem(5), out_specs=tuple(vmem(6)),
        compiler_params=pltpu.CompilerParams(vmem_limit_bytes=56 * 2**20),
        cost_estimate=LIGHT,
        name="attention_forward",
    )(qkv, cosine, sine, start, place)


def attention_backward(hl, kvl, q, k, v, att, lse, heads, cosine, sine, start, place):
    total = q.shape[0]
    block = 256 if total <= 1024 else 128
    qw, kw = hl * HEAD_DIM, kvl * HEAD_DIM
    shape = jax.ShapeDtypeStruct
    return pl.pallas_call(
        functools.partial(backward_kernel, hl, kvl, block),
        out_shape=(shape((total, qw + 2 * kw), BF16), shape((total, qw + 2 * kw), BF16)),
        in_specs=vmem(10), out_specs=tuple(vmem(2)),
        scratch_shapes=[
            pltpu.VMEM((total, qw), BF16), pltpu.VMEM((total, qw), F32),
            pltpu.VMEM((total, kw), F32), pltpu.VMEM((total, kw), F32),
        ],
        compiler_params=pltpu.CompilerParams(vmem_limit_bytes=56 * 2**20),
        cost_estimate=pl.CostEstimate(flops=4 * 10**10, bytes_accessed=1, transcendentals=0),
        name="attention_backward",
    )(q, k, v, att, lse, heads, cosine, sine, start, place)


def hidden_kernel(
    parts, n2_ref, dy_ref, up_ref, down_ref, hidden_ref, gate_grad_ref, up_grad_ref, grad_ref, grad_sum
):
    step = pl.program_id(0)
    wide = down_ref.shape[0] // parts
    total = None
    for part in range(parts):
        cols = slice(part * wide, (part + 1) * wide)
        both = dot(n2_ref[...], up_ref[part], ((1,), (0,)))
        gate, up = both[:, :wide], both[:, wide:]
        grad = dot(dy_ref[...], down_ref[cols, :], ((1,), (1,)))
        sigma = 1.0 / (1.0 + jnp.exp(-gate))
        silu = gate * sigma
        hidden_ref[:, cols] = (silu * up).astype(BF16)
        grad_gate = (grad * up * sigma * (1.0 + gate * (1.0 - sigma))).astype(BF16)
        grad_up = (grad * silu).astype(BF16)
        gate_grad_ref[:, cols] = grad_gate
        up_grad_ref[:, cols] = grad_up
        both = jnp.concatenate([grad_gate, grad_up], axis=1)
        both = dot(both, up_ref[part], ((1,), (1,)))
        total = both if total is None else total + both

    @pl.when(step == 0)
    def _():
        grad_sum[...] = total

    @pl.when(step > 0)
    def _():
        grad_sum[...] += total

    @pl.when(step == pl.num_programs(0) - 1)
    def _():
        grad_ref[...] = grad_sum[...].astype(BF16)


def feed_forward(n2, dy, w_gu, w_down, cost):
    rows, width = n2.shape
    ffs = w_down.shape[0]
    count, _, both = w_gu.shape
    wide = both // 2
    parts = max(1, 512 // wide)
    tile = parts * wide
    shape = jax.ShapeDtypeStruct
    whole = pl.BlockSpec((rows, width), lambda j: (0, 0), pipeline_mode=pl.Buffered(1))
    return pl.pallas_call(
        functools.partial(hidden_kernel, parts),
        grid=(count // parts,),
        in_specs=[
            whole,
            whole,
            pl.BlockSpec((parts, width, both), lambda j: (j, 0, 0)),
            pl.BlockSpec((tile, width), lambda j: (j, 0)),
        ],
        out_specs=[pl.BlockSpec((rows, tile), lambda j: (0, j))] * 3 + [whole],
        out_shape=[shape((rows, ffs), BF16)] * 3 + [shape((rows, width), BF16)],
        scratch_shapes=[pltpu.VMEM((rows, width), F32)],
        compiler_params=pltpu.CompilerParams(vmem_limit_bytes=60 * 2**20),
        cost_estimate=cost,
        name="feed_forward",
    )(n2, dy, w_gu, w_down)


def product_kernel(parts, *refs):
    lefts, rights = refs[:parts], refs[parts:-3]
    out_ref, done_ref, turned_ref = refs[-3:]
    count = len(rights) // parts
    step = pl.program_id(1)
    each = pl.num_programs(1) // count
    size = lefts[0].shape[0]

    @pl.when(step == 0)
    def _():
        for part in range(parts):
            turned_ref[:, part * size : (part + 1) * size] = lefts[part][...].T
        done_ref[...] = jnp.zeros_like(done_ref)

    for which in range(count):

        @pl.when((step >= which * each) & (step < (which + 1) * each))
        def _():
            value = 0.0
            for part in range(parts):
                turned = turned_ref[:, part * size : (part + 1) * size]
                value += dot(turned, rights[which * parts + part][...], ((1,), (0,)))
            out_ref[...] = value.astype(BF16).reshape(out_ref.shape)


def weight_gradient(lefts, rights, blocks, replicas, by_block):
    parts, (size, width) = len(lefts), lefts[0].shape
    cols = rights[0][0].shape[1]
    rows = width // blocks
    tile = min(1024, cols)
    each = cols // tile

    def place(which):
        return lambda i, j: (0, jnp.clip(j - which * each, 0, each - 1))

    if by_block:
        shape = (replicas, blocks, rows // replicas, len(rights) * cols)
        out_spec = pl.BlockSpec((replicas, 1, rows // replicas, tile), lambda i, j: (0, i, 0, j))
    else:
        shape = (width, len(rights) * cols)
        out_spec = pl.BlockSpec((rows, tile), lambda i, j: (i, j))
    return pl.pallas_call(
        functools.partial(product_kernel, parts),
        grid=(blocks, len(rights) * each),
        in_specs=[pl.BlockSpec((size, rows), lambda i, j: (0, i))] * parts
        + [pl.BlockSpec((size, tile), place(n)) for n in range(len(rights)) for _ in range(parts)],
        out_specs=[out_spec, pl.BlockSpec((8, 128), lambda i, j: (0, 0))],
        out_shape=[jax.ShapeDtypeStruct(shape, BF16), jax.ShapeDtypeStruct((8, 128), F32)],
        scratch_shapes=[pltpu.VMEM((rows, parts * size), BF16)],
        compiler_params=pltpu.CompilerParams(vmem_limit_bytes=56 * 2**20),
        cost_estimate=LIGHT,
        name="weight_gradient",
    )(*lefts, *[part for right in rights for part in right])


def mark(value):
    while value.ndim > 2:
        value = value[0]
    return value[:8, :128]


def after(value, *others, cost=LIGHT):
    leaves, tree = jax.tree.flatten(value)
    others = [mark(other) for other in jax.tree.leaves(others)]
    anywhere = pl.BlockSpec(memory_space=pl.ANY)
    tied = pl.pallas_call(
        lambda *refs: None,
        out_shape=[jax.ShapeDtypeStruct(leaf.shape, leaf.dtype) for leaf in leaves],
        in_specs=[anywhere] * (len(leaves) + len(others)),
        out_specs=[anywhere] * len(leaves),
        input_output_aliases={i: i for i in range(len(leaves))},
        cost_estimate=cost,
        name="after",
    )(*leaves, *others)
    return jax.tree.unflatten(tree, tied)


def pair_kernel(odd_ref, own_ref, low_ref, high_ref, out_ref):
    size = own_ref.shape[0]
    out_ref[:size, :] = own_ref[...]

    @pl.when(odd_ref[0] == 0)
    def _():
        out_ref[size:, :] = high_ref[...]

    @pl.when(odd_ref[0] != 0)
    def _():
        out_ref[size:, :] = low_ref[...]


class Line:
    def __init__(self, count):
        self.count = count
        self.me = lax.axis_index("group")

    def swap(self, value, slot):
        return lax.ppermute(value, "group", [(i, i ^ slot) for i in range(self.count)])

    def at(self, value, slot, axis=0):
        return lax.dynamic_index_in_dim(value, self.me ^ slot, axis, keepdims=False)

    def exchange(self, slots):
        return [slots[0]] + [self.swap(slots[k], k) for k in range(1, self.count)]

    def ordered(self, slots):
        return [self.pick(slots, j) for j in range(self.count)]

    def pick(self, slots, device):
        value = slots[0]
        for k in range(1, self.count):
            value = jnp.where(self.me == device ^ k, slots[k], value)
        return value

    def near(self, begun):
        (own, low), (_, high) = begun
        size, cols = own.shape
        return pl.pallas_call(
            pair_kernel,
            out_shape=jax.ShapeDtypeStruct((2 * size, cols), own.dtype),
            in_specs=[pl.BlockSpec(memory_space=pltpu.SMEM)] + vmem(3),
            out_specs=pl.BlockSpec(memory_space=pltpu.VMEM),
            compiler_params=pltpu.CompilerParams(vmem_limit_bytes=16 * 2**20),
            cost_estimate=LIGHT,
            name="pair",
        )(self.me.reshape(1) % 2, own, low, high)

    def gather(self, value, gates=(), hops=None, begun=None):
        count = self.count
        low, high = begun if begun else ([value], [value])
        low, high = list(low), list(high)
        for hop in range(len(low), (hops or count - 1) + 1):
            moving = (low[-1], high[-1])
            if hop <= len(gates) and gates[hop - 1] is not None:
                if hop == 1:
                    moving = (after(value, gates[0]),) * 2
                else:
                    moving = low[-1], high[-1] = after(moving, gates[hop - 1])
            up = [(i, i + 1) for i in range(hop - 1, count - 1)]
            down = [(i + 1, i) for i in range(count - hop)]
            low.append(lax.ppermute(moving[0], "group", up))
            high.append(lax.ppermute(moving[1], "group", down))
        if hops:
            return low, high
        self.last = (low[1:], high[1:])
        slots = [value]
        for k in range(1, count):
            chosen = None
            for device in range(count):
                source = device ^ k
                came = high[source - device] if source > device else low[device - source]
                chosen = came if chosen is None else jnp.where(self.me == device, came, chosen)
            slots.append(chosen)
        return slots

    def scatter_hop(self, slots, came, hop, gate=()):
        count = self.count
        up = [(i, i + 1) for i in range(count - hop)]
        down = [(i + 1, i) for i in range(hop - 1, count - 1)]
        moving = [self.pick_far(slots, hop), self.pick_far(slots, -hop)]
        if came:
            moving = [mine + part for mine, part in zip(moving, came)]
        if gate:
            moving = after(moving, gate)
        return (lax.ppermute(moving[0], "group", up), lax.ppermute(moving[1], "group", down))

    def scatter_sum(self, slots):
        came = None
        for hop in range(self.count - 1, 0, -1):
            came = self.scatter_hop(slots, came, hop)
        return slots[0].astype(F32) + came[0].astype(F32) + came[1].astype(F32)

    def pick_far(self, slots, distance):
        chosen = slots[1]
        for device in range(self.count):
            other = device + distance
            if 0 <= other < self.count:
                chosen = jnp.where(self.me == device, slots[device ^ other], chosen)
        return chosen


def gather_plane(value, replicas, me):
    bits = [1 << i for i in range(1, replicas.bit_length() - 1)]
    middle = value.shape[0] // 2

    def swap(part, bit):
        return lax.ppermute(part, "replica", [(i, i ^ bit) for i in range(replicas)])

    halves = []
    for half, order in ((value[:middle], bits), (value[middle:], bits[::-1])):
        held, places = half[None], [0]
        for bit in order:
            held = jnp.concatenate([held, swap(held, bit)])
            places = places + [place ^ bit for place in places]
        halves.append(jnp.stack([held[places.index(2 * i)] for i in range(replicas // 2)]))
    held = jnp.concatenate(halves, axis=1)
    held = jnp.stack([held, swap(held, 1)], axis=1)
    held = held.reshape(replicas, *value.shape)
    return jnp.stack(
        [lax.dynamic_index_in_dim(held, me ^ i, 0, keepdims=False) for i in range(replicas)]
    )


def local(
    tokens,
    cotangent,
    lengths,
    packing,
    attn_gain,
    w_query,
    w_key_value,
    w_out,
    mlp_gain,
    w_gate_up,
    w_down,
):
    ntok, width = tokens.shape
    total = packing.shape[1]
    groups = total // ntok
    shard = w_query.shape[0]
    replicas = lax.axis_size("replica")
    rows = shard // replicas
    kvl = KV_HEADS // groups
    hl = HEADS // groups
    qw = hl * HEAD_DIM
    kw = kvl * HEAD_DIM
    qkvw = qw + 2 * kw
    ff = w_gate_up.shape[2]
    ffs = ff // groups
    me_r = lax.axis_index("replica")
    line = Line(groups)

    def own_rows(value):
        return lax.dynamic_slice_in_dim(value, me_r * rows, rows)

    def over_plane(value):
        return lax.all_gather(value, "replica", axis=0)

    wq_rows = own_rows(w_query).reshape(rows, groups, qw)
    wkv_rows = own_rows(w_key_value).reshape(rows, 2, groups, kw)
    wkv_rows = wkv_rows.transpose(0, 2, 1, 3).reshape(rows, groups, 2 * kw)
    qkv_rows = jnp.concatenate([wq_rows, wkv_rows], axis=2)
    ffr = ffs // replicas
    gu_cols = []
    for k in range(groups):
        first = (line.me ^ k) * ffs + me_r * ffr
        part = lax.dynamic_slice(w_gate_up, (0, 0, first), (shard, 2, ffr))
        gu_cols.append(jnp.concatenate([part[:, 0], part[:, 1]], axis=1))
    gu_cols = jnp.stack(gu_cols)
    out_cols = lax.dynamic_slice_in_dim(w_out, me_r * (width // replicas), width // replicas, 1)

    w_qkv = line.exchange([line.at(qkv_rows, k, 1) for k in range(groups)])
    gains = jnp.stack([attn_gain, mlp_gain])
    gains = jnp.concatenate(line.ordered(line.exchange([gains] * groups)), axis=1)
    gain1, gain2 = gains[0], gains[1]
    w_out_cols = line.exchange([out_cols] * groups)
    x_hops = line.gather(tokens, (), 1)
    x_came = [part[1] for part in x_hops]
    w_qkv, w_out_cols[1:], x_came = after((w_qkv, w_out_cols[1:], x_came), gu_cols)
    x_hops = [[tokens, part] for part in x_came]
    seats = jnp.arange(total, dtype=jnp.int32)
    _, position = stream_meta(lengths[0], seats)
    start = (seats - position)[:, None]
    angles = position.astype(F32)[:, None] * frequencies(HEAD_DIM)[None, :]
    copies = 128 // HEAD_DIM
    cosine = jnp.tile(jnp.cos(angles), (1, 2 * copies))
    sine = jnp.sin(angles)
    sine = jnp.tile(jnp.concatenate([-sine, sine], axis=1), (1, copies))
    seat = packing.reshape(groups, ntok)
    seat = jnp.concatenate([line.at(seat, k) for k in range(groups)])
    place = (seat[None, :] == seats[:, None]).astype(BF16)
    w_qkv = over_plane(jnp.stack(line.ordered(w_qkv)))
    w_qkv = jnp.swapaxes(w_qkv, 0, 1).reshape(width, qkvw)
    x_slots = line.gather(tokens, (), 0, x_hops)
    x_last = [part[-1] for part in line.last]
    w_out_cols = over_plane(jnp.concatenate(w_out_cols))
    gu_cols = after(gu_cols, x_last)
    gu_cols = line.exchange([gu_cols[k] for k in range(groups)])
    dy_hops = line.gather(cotangent, (x_last,), 1)

    def normed(value):
        value = value.astype(F32)
        return (value * inverse_rms(value) * gain1).astype(BF16)

    normed1 = jnp.concatenate([normed(value) for value in x_slots])
    normed1 = dot(place, normed1, ((1,), (0,))).astype(BF16)
    qkv = dot(normed1, w_qkv, ((1,), (0,)))
    q_rot, k_rot, values, attended, lse, attended_low = attention_forward(
        hl, kvl, qkv, cosine, sine, start, place
    )

    def cut(value):
        return [value[k * ntok : (k + 1) * ntok] for k in range(groups)]

    dy_near = dy_hops
    attended_low = after(attended_low, [part[1] for part in dy_hops])
    own_attended = line.exchange(cut(attended_low))
    w_gu = over_plane(jnp.concatenate(line.ordered(after(gu_cols, attended_low))))
    x_own = tokens.astype(F32)
    own_attended_all = jnp.concatenate(own_attended, axis=1)
    h1 = lax.dot_general(own_attended_all, w_out_cols, (((1,), (1,)), ((), ())), preferred_element_type=F32)
    h1 = x_own + h1.reshape(ntok, width)
    inv2 = inverse_rms(h1)
    unit2 = h1 * inv2
    normed2 = (unit2 * gain2).astype(BF16)
    n2_near = line.gather(normed2, (), 1)
    dy_hops = line.gather(cotangent, (None, own_attended[1:]), 2, dy_hops)
    near_parts = [line.near(n2_near), line.near(dy_near)]

    half = groups // 2
    if half > 2:
        n2, dy = line.gather(normed2, (), 0, n2_near), line.gather(cotangent, (), 0, dy_hops)
        near_parts = [jnp.concatenate(part[:half]) for part in (n2, dy)]
    near = feed_forward(*near_parts, w_gu, w_down, HEAVY)
    if half == 2:
        n2 = line.gather(normed2, (None, None, near[3]), 0, n2_near)
        dy_hops = line.gather(cotangent, (None, None, n2_near), 3, dy_hops)
        for part, last in zip(dy_hops, after([part[-1] for part in dy_hops], near[3])):
            part[-1] = last
        dy = line.gather(cotangent, (), 0, dy_hops)
    n2_parts = [near_parts[0], jnp.concatenate(n2[half:])]
    dy_parts = [near_parts[1], jnp.concatenate(dy[half:])]
    n2_parts[1] = after(n2_parts[1], near[3])
    far = feed_forward(n2_parts[1], dy_parts[1], w_gu, w_down, LIGHT)
    grad_n2 = line.exchange(cut(near[3])[:half] + cut(far[3])[:half])

    def sum_plane(value):
        return lax.psum_scatter(value, "replica", scatter_dimension=0)

    hidden = [near[0], far[0]]
    down_grad, down_done = weight_gradient(hidden, [dy_parts], groups, replicas, False)
    n2_parts[0] = after(n2_parts[0], down_done)
    gu_grad, gu_done = weight_gradient(
        n2_parts, [[near[1], far[1]], [near[2], far[2]]], groups, replicas, True
    )
    down_grad = sum_plane(down_grad.reshape(replicas, ffs // replicas, width))
    gu_grad = gu_grad.reshape(replicas, groups * rows, 2 * ffs)
    gu_grad = sum_plane(gu_grad).reshape(groups, rows, 2 * ffs)

    grad_n2 = after(grad_n2, gu_done, cost=HEAVY)
    grad_n2 = sum([part.astype(F32) for part in grad_n2])
    gain2_grad = jnp.sum(grad_n2 * unit2, axis=0)
    grad_h1 = cotangent.astype(F32) + rms_norm_backward(grad_n2, unit2, inv2, gain2)
    grad_attn = grad_h1.astype(BF16)
    grad_heads = lax.dot_general(
        grad_attn.reshape(ntok, replicas, width // replicas),
        w_out_cols,
        (((1, 2), (0, 2)), ((), ())),
        preferred_element_type=F32,
    ).astype(BF16)
    heads_there = grad_heads
    grad_heads = line.exchange([grad_heads[:, k * qw : (k + 1) * qw] for k in range(groups)])
    grad_heads = jnp.concatenate(grad_heads)
    ga_hops = line.gather(grad_attn, (grad_heads,), 1)
    grad_qkv, own_qkv = attention_backward(
        hl, kvl, q_rot, k_rot, values, attended, lse, grad_heads, cosine, sine, start, place
    )
    down = [dot(after(part, own_qkv), w_down, ((1,), (0,))).astype(BF16) for part in hidden]
    down = cut(down[0])[:half] + cut(down[1])[:half]
    own_qkv = after(own_qkv, [part[1] for part in ga_hops])
    qkv_grad = dot(normed1, grad_qkv, ((0,), (0,))).astype(BF16)
    grad_n1 = dot(own_qkv, w_qkv, ((1,), (1,))).astype(BF16)

    def by_group(value):
        return line.exchange([line.at(value, k) for k in range(groups)])

    qkv_grad = qkv_grad.reshape(groups, replicas, rows, qkvw).transpose(1, 2, 0, 3)
    qkv_grad = qkv_grad.reshape(replicas, rows, groups * qkvw)
    n1_slots, n1_hops = cut(grad_n1), []
    for i in range(groups - 1):
        came = n1_hops[-1] if n1_hops else None
        gate = [part[-1] for part in ga_hops] if i else ()
        n1_hops.append(line.scatter_hop(n1_slots, came, groups - 1 - i, gate))
        if i + 2 < groups:
            gates = [None] * (i + 1) + [came if i else own_qkv]
            ga_hops = line.gather(grad_attn, gates, i + 2, ga_hops)
    gu_grad, down_grad, qkv_grad = after((gu_grad, down_grad, qkv_grad), n1_hops[0])
    qkv_grad = sum_plane(qkv_grad)
    down_grad = over_plane(down_grad).reshape(ffs, width)
    gu_grad = by_group(after(gu_grad, n1_hops[-2]))
    grad_n1 = sum(part.astype(F32) for part in (n1_slots[0], *n1_hops[-1]))
    grad_attn_all = line.gather(grad_attn, (), 0, ga_hops)
    inv1 = inverse_rms(x_own)
    unit1 = x_own * inv1
    gain1_grad = jnp.sum(grad_n1 * unit1, axis=0)
    x_grad = (grad_h1 + rms_norm_backward(grad_n1, unit1, inv1, gain1)).astype(BF16)

    grad_attn_all = jnp.concatenate(after(grad_attn_all, grad_n1))
    out_grad = dot(attended_low, grad_attn_all, ((0,), (0,))).astype(BF16)
    gain_grads = jnp.stack([gain1_grad, gain2_grad]).reshape(2, groups, replicas, rows)
    gain_grads = gain_grads.transpose(2, 3, 1, 0).astype(BF16)
    gain_grads = jnp.pad(gain_grads, ((0, 0), (0, 0), (0, 0), (0, 128 - 2)))
    out_grad = out_grad.reshape(replicas, rows, width)
    gain_grads = gain_grads.reshape(replicas, rows, groups * 128)
    out_grad = jnp.concatenate([out_grad, gain_grads], axis=2)
    out_grad = sum_plane(after(out_grad, down_grad, qkv_grad))
    y_hops = []
    for hop in range(groups - 1, 0, -1):
        gate = (n1_hops[-1], gu_grad[1:], ())[min(len(y_hops), 2)]
        y_hops.append(line.scatter_hop(down, y_hops[-1] if y_hops else None, hop, gate))
    mixed = (h1 + sum(part.astype(F32) for part in (down[0], *y_hops[-1]))).astype(BF16)

    gu_grad = line.ordered(gu_grad)
    gu_grad = jnp.concatenate([part.reshape(rows, 2, ffs) for part in gu_grad], axis=2)
    gu_grad = over_plane(after(gu_grad, out_grad, y_hops[0]))

    grads = jnp.concatenate(
        [qkv_grad.reshape(rows, groups, qkvw), out_grad[:, width:].reshape(rows, groups, 128)], axis=2
    )
    grads = by_group(jnp.swapaxes(grads, 0, 1))
    gain_grads = sum([part[:, qkvw:].astype(F32) for part in grads]).astype(BF16)
    grads = line.ordered(grads)
    grads = [part[:, :qw] for part in grads] + [
        part[:, qw + j * kw : qw + (j + 1) * kw] for j in range(2) for part in grads
    ]
    grads = jnp.concatenate(grads + [out_grad[:, :width], gain_grads], axis=1)
    grads = gather_plane(grads, replicas, me_r)
    gu_grad = gu_grad.reshape(shard, 2, ff).astype(F32)
    down_grad = down_grad.astype(F32)
    grads = grads.reshape(shard, -1).astype(F32)
    q_grad = grads[:, :width]
    kv_grad = grads[:, width : width + 2 * groups * kw].reshape(shard, 2, groups * kw)
    out_grad = grads[:, width + 2 * groups * kw : 2 * width + 2 * groups * kw]
    gain_grads = grads[:, -128:]
    return (
        mixed,
        x_grad,
        gain_grads[:, 0],
        q_grad,
        kv_grad,
        out_grad,
        gain_grads[:, 1],
        gu_grad,
        down_grad,
    )


def solution(mesh):
    rows = P(("replica", "group"), None)
    flat, two, three = P("group"), P("group", None), P("group", None, None)
    return jax.shard_map(
        local,
        mesh=mesh,
        in_specs=(
            rows,
            rows,
            P("replica", None),
            P("replica", None),
            flat,
            two,
            three,
            two,
            flat,
            three,
            two,
        ),
        out_specs=(rows, rows, flat, two, three, two, flat, three, two),
        check_vma=False,
    )
```

```python
import functools
import math

import jax
import jax.numpy as jnp
from jax import lax
from jax.experimental import pallas as pl
from jax.experimental.pallas import tpu as pltpu
from jax.sharding import PartitionSpec as P

HEADS = 32
KV_HEADS = 8
HEAD_DIM = 64
EPS = 1e-05
NEG = -1e30
F32 = jnp.float32
BF16 = jnp.bfloat16
LIGHT = pl.CostEstimate(flops=1, bytes_accessed=1, transcendentals=0)
HEAVY = pl.CostEstimate(flops=3 * 10**11, bytes_accessed=1, transcendentals=0)


def frequencies(head_size):
    half = head_size // 2
    expo = jnp.arange(half).astype(F32) * (2.0 / head_size)
    base = jnp.power(F32(500000.0), -expo)
    wavelen = 2.0 * math.pi / base
    smooth = (8192.0 / wavelen - 1.0) / 3.0
    middle = (1.0 - smooth) * base / 32.0 + smooth * base
    return jnp.where(wavelen < 2048.0, base, jnp.where(wavelen > 8192.0, base / 32.0, middle))


def stream_meta(lengths_row, stream):
    ends = jnp.cumsum(lengths_row)
    past = ends[None, :] <= stream[:, None]
    segment = jnp.sum(past.astype(jnp.int32), axis=1)
    before = jnp.sum(jnp.where(past, lengths_row[None, :], 0), axis=1)
    return (segment, stream - before)


def inverse_rms(value):
    return lax.rsqrt(jnp.mean(value * value, axis=-1, keepdims=True) + EPS)


def rms_norm_backward(grad, unit, inverse, gain):
    scaled = grad * gain
    return inverse * (scaled - unit * jnp.mean(scaled * unit, axis=-1, keepdims=True))


def swap_halves(value):
    wide = value.shape[-1]
    lane = lax.broadcasted_iota(jnp.int32, value.shape, 1)
    low = lane % HEAD_DIM < HEAD_DIM // 2
    return jnp.where(
        low,
        pltpu.roll(value, wide - HEAD_DIM // 2, 1),
        pltpu.roll(value, HEAD_DIM // 2, 1),
    )


def rotate(value, cosine, sine, width):
    copies = value.shape[-1] // cosine.shape[-1]
    cosine = jnp.concatenate([cosine] * copies, axis=1)
    sine = jnp.concatenate([sine] * copies, axis=1)
    lane = lax.broadcasted_iota(jnp.int32, value.shape, 1)
    return jnp.where(lane < width, value * cosine + swap_halves(value) * sine, value)


def dot(left, right, dims):
    return lax.dot_general(left, right, (dims, ((), ())), preferred_element_type=F32)


def stacked(ref, rows, first, share):
    return jnp.concatenate(
        [ref[rows, (first + h) * HEAD_DIM : (first + h + 1) * HEAD_DIM] for h in range(share)], axis=0
    )


def bias_of(start, row0, block, keys):
    row = row0 + lax.broadcasted_iota(jnp.int32, (block, keys), 0)
    col = lax.broadcasted_iota(jnp.int32, (block, keys), 1)
    return jnp.where((col <= row) & (col >= start), 0.0, NEG).astype(F32)


def forward_kernel(
    hl, kvl, block, qkv_ref, cos_ref, sin_ref, start_ref, place_ref,
    q_ref, k_ref, v_ref, att_ref, lse_ref, low_ref,
):
    total = qkv_ref.shape[0]
    share = hl // kvl
    qw, kw = hl * HEAD_DIM, kvl * HEAD_DIM
    for row0 in range(0, total, block):
        rows = pl.ds(row0, block)
        turned = rotate(qkv_ref[rows, :], cos_ref[rows, :], sin_ref[rows, :], qw + kw)
        q_ref[rows, :] = (turned[:, :qw].astype(BF16) * HEAD_DIM ** (-0.5)).astype(BF16)
        k_ref[rows, :] = turned[:, qw : qw + kw].astype(BF16)
        v_ref[rows, :] = turned[:, qw + kw :].astype(BF16)
    for row0 in range(0, total, block):
        rows = pl.ds(row0, block)
        keys = row0 + block
        bias = bias_of(start_ref[rows, :], row0, block, keys)
        for kv in range(kvl):
            cols = slice(kv * HEAD_DIM, (kv + 1) * HEAD_DIM)
            query = stacked(q_ref, rows, kv * share, share)
            raw = dot(query, k_ref[:keys, cols], ((1,), (1,)))
            raw = (raw.reshape(share, block, keys) + bias[None]).reshape(share * block, keys)
            top = jnp.max(raw, axis=-1, keepdims=True)
            probs = jnp.exp(raw - top)
            total_p = jnp.sum(probs, axis=-1, keepdims=True)
            out = dot(probs.astype(BF16), v_ref[:keys, cols], ((1,), (0,))) / total_p
            lse = top + jnp.log(total_p)
            for h in range(share):
                head = kv * share + h
                part = slice(h * block, (h + 1) * block)
                att_ref[rows, head * HEAD_DIM : (head + 1) * HEAD_DIM] = out[part]
                lse_ref[rows, head : head + 1] = lse[part]
    low_ref[...] = dot(place_ref[...], att_ref[...].astype(BF16), ((0,), (0,))).astype(BF16)


def backward_kernel(
    hl, kvl, block, q_ref, k_ref, v_ref, att_ref, lse_ref, heads_ref, cos_ref, sin_ref, start_ref, place_ref,
    grad_ref, native_ref, gh_ref, gq_ref, gk_ref, gv_ref,
):
    total = q_ref.shape[0]
    share = hl // kvl
    qw, kw = hl * HEAD_DIM, kvl * HEAD_DIM
    gh_ref[...] = dot(place_ref[...], heads_ref[...], ((1,), (0,))).astype(BF16)
    gk_ref[...] = jnp.zeros_like(gk_ref)
    gv_ref[...] = jnp.zeros_like(gv_ref)
    for row0 in range(0, total, block):
        rows = pl.ds(row0, block)
        keys = row0 + block
        bias = bias_of(start_ref[rows, :], row0, block, keys)
        for kv in range(kvl):
            cols = slice(kv * HEAD_DIM, (kv + 1) * HEAD_DIM)
            query = stacked(q_ref, rows, kv * share, share)
            heads = stacked(gh_ref, rows, kv * share, share)
            att = stacked(att_ref, rows, kv * share, share)
            delta = jnp.sum(heads.astype(F32) * att, axis=-1, keepdims=True)
            lse = jnp.concatenate(
                [lse_ref[rows, kv * share + h : kv * share + h + 1] for h in range(share)], axis=0
            )
            raw = dot(query, k_ref[:keys, cols], ((1,), (1,)))
            raw = (raw.reshape(share, block, keys) + bias[None]).reshape(share * block, keys)
            probs = jnp.exp(raw - lse)
            grad_probs = dot(heads, v_ref[:keys, cols], ((1,), (1,)))
            scores = (probs * (grad_probs - delta)).astype(BF16)
            out = dot(scores, k_ref[:keys, cols], ((1,), (0,))) * HEAD_DIM ** (-0.5)
            for h in range(share):
                head = kv * share + h
                gq_ref[rows, head * HEAD_DIM : (head + 1) * HEAD_DIM] = out[h * block : (h + 1) * block]
            gk_ref[:keys, cols] += dot(scores, query, ((0,), (0,)))
            gv_ref[:keys, cols] += dot(probs.astype(BF16), heads, ((0,), (0,)))
    for row0 in range(0, total, block):
        rows = pl.ds(row0, block)
        grad = jnp.concatenate([gq_ref[rows, :], gk_ref[rows, :], gv_ref[rows, :]], axis=1)
        grad_ref[rows, :] = rotate(grad, cos_ref[rows, :], -sin_ref[rows, :], qw + kw).astype(BF16)
    native_ref[...] = dot(place_ref[...], grad_ref[...], ((0,), (0,))).astype(BF16)


def vmem(count):
    return [pl.BlockSpec(memory_space=pltpu.VMEM)] * count


def attention_forward(hl, kvl, qkv, cosine, sine, start, place):
    total = qkv.shape[0]
    block = 256 if total <= 1024 else 128
    qw, kw = hl * HEAD_DIM, kvl * HEAD_DIM
    shape = jax.ShapeDtypeStruct
    return pl.pallas_call(
        functools.partial(forward_kernel, hl, kvl, block),
        out_shape=(
            shape((total, qw), BF16), shape((total, kw), BF16), shape((total, kw), BF16),
            shape((total, qw), F32), shape((total, 128), F32), shape((total, qw), BF16),
        ),
        in_specs=vmem(5), out_specs=tuple(vmem(6)),
        compiler_params=pltpu.CompilerParams(vmem_limit_bytes=56 * 2**20),
        cost_estimate=LIGHT,
        name="attention_forward",
    )(qkv, cosine, sine, start, place)


def attention_backward(hl, kvl, q, k, v, att, lse, heads, cosine, sine, start, place):
    total = q.shape[0]
    block = 256 if total <= 1024 else 128
    qw, kw = hl * HEAD_DIM, kvl * HEAD_DIM
    shape = jax.ShapeDtypeStruct
    return pl.pallas_call(
        functools.partial(backward_kernel, hl, kvl, block),
        out_shape=(shape((total, qw + 2 * kw), BF16), shape((total, qw + 2 * kw), BF16)),
        in_specs=vmem(10), out_specs=tuple(vmem(2)),
        scratch_shapes=[
            pltpu.VMEM((total, qw), BF16), pltpu.VMEM((total, qw), F32),
            pltpu.VMEM((total, kw), F32), pltpu.VMEM((total, kw), F32),
        ],
        compiler_params=pltpu.CompilerParams(vmem_limit_bytes=56 * 2**20),
        cost_estimate=pl.CostEstimate(flops=4 * 10**10, bytes_accessed=1, transcendentals=0),
        name="attention_backward",
    )(q, k, v, att, lse, heads, cosine, sine, start, place)


def hidden_kernel(
    parts, n2_ref, dy_ref, up_ref, down_ref, hidden_ref, gate_grad_ref, up_grad_ref, grad_ref, grad_sum
):
    step = pl.program_id(0)
    wide = down_ref.shape[0] // parts
    total = None
    for part in range(parts):
        cols = slice(part * wide, (part + 1) * wide)
        both = dot(n2_ref[...], up_ref[part], ((1,), (0,)))
        gate, up = both[:, :wide], both[:, wide:]
        grad = dot(dy_ref[...], down_ref[cols, :], ((1,), (1,)))
        sigma = 1.0 / (1.0 + jnp.exp(-gate))
        silu = gate * sigma
        hidden_ref[:, cols] = (silu * up).astype(BF16)
        grad_gate = (grad * up * sigma * (1.0 + gate * (1.0 - sigma))).astype(BF16)
        grad_up = (grad * silu).astype(BF16)
        gate_grad_ref[:, cols] = grad_gate
        up_grad_ref[:, cols] = grad_up
        both = jnp.concatenate([grad_gate, grad_up], axis=1)
        both = dot(both, up_ref[part], ((1,), (1,)))
        total = both if total is None else total + both

    @pl.when(step == 0)
    def _():
        grad_sum[...] = total

    @pl.when(step > 0)
    def _():
        grad_sum[...] += total

    @pl.when(step == pl.num_programs(0) - 1)
    def _():
        grad_ref[...] = grad_sum[...].astype(BF16)


def feed_forward(n2, dy, w_gu, w_down, cost):
    rows, width = n2.shape
    ffs = w_down.shape[0]
    count, _, both = w_gu.shape
    wide = both // 2
    parts = max(1, 512 // wide)
    tile = parts * wide
    shape = jax.ShapeDtypeStruct
    whole = pl.BlockSpec((rows, width), lambda j: (0, 0), pipeline_mode=pl.Buffered(1))
    return pl.pallas_call(
        functools.partial(hidden_kernel, parts),
        grid=(count // parts,),
        in_specs=[
            whole,
            whole,
            pl.BlockSpec((parts, width, both), lambda j: (j, 0, 0)),
            pl.BlockSpec((tile, width), lambda j: (j, 0)),
        ],
        out_specs=[pl.BlockSpec((rows, tile), lambda j: (0, j))] * 3 + [whole],
        out_shape=[shape((rows, ffs), BF16)] * 3 + [shape((rows, width), BF16)],
        scratch_shapes=[pltpu.VMEM((rows, width), F32)],
        compiler_params=pltpu.CompilerParams(vmem_limit_bytes=60 * 2**20),
        cost_estimate=cost,
        name="feed_forward",
    )(n2, dy, w_gu, w_down)


def product_kernel(parts, *refs):
    lefts, rights = refs[:parts], refs[parts:-3]
    out_ref, done_ref, turned_ref = refs[-3:]
    count = len(rights) // parts
    step = pl.program_id(1)
    each = pl.num_programs(1) // count
    size = lefts[0].shape[0]

    @pl.when(step == 0)
    def _():
        for part in range(parts):
            turned_ref[:, part * size : (part + 1) * size] = lefts[part][...].T
        done_ref[...] = jnp.zeros_like(done_ref)

    for which in range(count):

        @pl.when((step >= which * each) & (step < (which + 1) * each))
        def _():
            value = 0.0
            for part in range(parts):
                turned = turned_ref[:, part * size : (part + 1) * size]
                value += dot(turned, rights[which * parts + part][...], ((1,), (0,)))
            out_ref[...] = value.astype(BF16).reshape(out_ref.shape)


def weight_gradient(lefts, rights, blocks, replicas, by_block):
    parts, (size, width) = len(lefts), lefts[0].shape
    cols = rights[0][0].shape[1]
    rows = width // blocks
    tile = min(1024, cols)
    each = cols // tile

    def place(which):
        return lambda i, j: (0, jnp.clip(j - which * each, 0, each - 1))

    if by_block:
        shape = (replicas, blocks, rows // replicas, len(rights) * cols)
        out_spec = pl.BlockSpec((replicas, 1, rows // replicas, tile), lambda i, j: (0, i, 0, j))
    else:
        shape = (width, len(rights) * cols)
        out_spec = pl.BlockSpec((rows, tile), lambda i, j: (i, j))
    return pl.pallas_call(
        functools.partial(product_kernel, parts),
        grid=(blocks, len(rights) * each),
        in_specs=[pl.BlockSpec((size, rows), lambda i, j: (0, i))] * parts
        + [pl.BlockSpec((size, tile), place(n)) for n in range(len(rights)) for _ in range(parts)],
        out_specs=[out_spec, pl.BlockSpec((8, 128), lambda i, j: (0, 0))],
        out_shape=[jax.ShapeDtypeStruct(shape, BF16), jax.ShapeDtypeStruct((8, 128), F32)],
        scratch_shapes=[pltpu.VMEM((rows, parts * size), BF16)],
        compiler_params=pltpu.CompilerParams(vmem_limit_bytes=56 * 2**20),
        cost_estimate=LIGHT,
        name="weight_gradient",
    )(*lefts, *[part for right in rights for part in right])


def mark(value):
    while value.ndim > 2:
        value = value[0]
    return value[:8, :128]


def after(value, *others, cost=LIGHT):
    leaves, tree = jax.tree.flatten(value)
    others = [mark(other) for other in jax.tree.leaves(others)]
    anywhere = pl.BlockSpec(memory_space=pl.ANY)
    tied = pl.pallas_call(
        lambda *refs: None,
        out_shape=[jax.ShapeDtypeStruct(leaf.shape, leaf.dtype) for leaf in leaves],
        in_specs=[anywhere] * (len(leaves) + len(others)),
        out_specs=[anywhere] * len(leaves),
        input_output_aliases={i: i for i in range(len(leaves))},
        cost_estimate=cost,
        name="after",
    )(*leaves, *others)
    return jax.tree.unflatten(tree, tied)


def pair_kernel(odd_ref, own_ref, low_ref, high_ref, out_ref):
    size = own_ref.shape[0]
    out_ref[:size, :] = own_ref[...]

    @pl.when(odd_ref[0] == 0)
    def _():
        out_ref[size:, :] = high_ref[...]

    @pl.when(odd_ref[0] != 0)
    def _():
        out_ref[size:, :] = low_ref[...]


class Line:
    def __init__(self, count):
        self.count = count
        self.me = lax.axis_index("group")

    def swap(self, value, slot):
        return lax.ppermute(value, "group", [(i, i ^ slot) for i in range(self.count)])

    def at(self, value, slot, axis=0):
        return lax.dynamic_index_in_dim(value, self.me ^ slot, axis, keepdims=False)

    def exchange(self, slots):
        return [slots[0]] + [self.swap(slots[k], k) for k in range(1, self.count)]

    def ordered(self, slots):
        return [self.pick(slots, j) for j in range(self.count)]

    def pick(self, slots, device):
        value = slots[0]
        for k in range(1, self.count):
            value = jnp.where(self.me == device ^ k, slots[k], value)
        return value

    def near(self, begun):
        (own, low), (_, high) = begun
        size, cols = own.shape
        return pl.pallas_call(
            pair_kernel,
            out_shape=jax.ShapeDtypeStruct((2 * size, cols), own.dtype),
            in_specs=[pl.BlockSpec(memory_space=pltpu.SMEM)] + vmem(3),
            out_specs=pl.BlockSpec(memory_space=pltpu.VMEM),
            compiler_params=pltpu.CompilerParams(vmem_limit_bytes=16 * 2**20),
            cost_estimate=LIGHT,
            name="pair",
        )(self.me.reshape(1) % 2, own, low, high)

    def gather(self, value, gates=(), hops=None, begun=None):
        count = self.count
        low, high = begun if begun else ([value], [value])
        low, high = list(low), list(high)
        for hop in range(len(low), (hops or count - 1) + 1):
            moving = (low[-1], high[-1])
            if hop <= len(gates) and gates[hop - 1] is not None:
                if hop == 1:
                    moving = (after(value, gates[0]),) * 2
                else:
                    moving = low[-1], high[-1] = after(moving, gates[hop - 1])
            up = [(i, i + 1) for i in range(hop - 1, count - 1)]
            down = [(i + 1, i) for i in range(count - hop)]
            low.append(lax.ppermute(moving[0], "group", up))
            high.append(lax.ppermute(moving[1], "group", down))
        if hops:
            return low, high
        self.last = (low[1:], high[1:])
        slots = [value]
        for k in range(1, count):
            chosen = None
            for device in range(count):
                source = device ^ k
                came = high[source - device] if source > device else low[device - source]
                chosen = came if chosen is None else jnp.where(self.me == device, came, chosen)
            slots.append(chosen)
        return slots

    def scatter_hop(self, slots, came, hop, gate=()):
        count = self.count
        up = [(i, i + 1) for i in range(count - hop)]
        down = [(i + 1, i) for i in range(hop - 1, count - 1)]
        moving = [self.pick_far(slots, hop), self.pick_far(slots, -hop)]
        if came:
            moving = [mine + part for mine, part in zip(moving, came)]
        if gate:
            moving = after(moving, gate)
        return (lax.ppermute(moving[0], "group", up), lax.ppermute(moving[1], "group", down))

    def scatter_sum(self, slots):
        came = None
        for hop in range(self.count - 1, 0, -1):
            came = self.scatter_hop(slots, came, hop)
        return slots[0].astype(F32) + came[0].astype(F32) + came[1].astype(F32)

    def pick_far(self, slots, distance):
        chosen = slots[1]
        for device in range(self.count):
            other = device + distance
            if 0 <= other < self.count:
                chosen = jnp.where(self.me == device, slots[device ^ other], chosen)
        return chosen


def gather_plane(value, replicas, me):
    bits = [1 << i for i in range(1, replicas.bit_length() - 1)]
    middle = value.shape[0] // 2

    def swap(part, bit):
        return lax.ppermute(part, "replica", [(i, i ^ bit) for i in range(replicas)])

    halves = []
    for half, order in ((value[:middle], bits), (value[middle:], bits[::-1])):
        held, places = half[None], [0]
        for bit in order:
            held = jnp.concatenate([held, swap(held, bit)])
            places = places + [place ^ bit for place in places]
        halves.append(jnp.stack([held[places.index(2 * i)] for i in range(replicas // 2)]))
    held = jnp.concatenate(halves, axis=1)
    held = jnp.stack([held, swap(held, 1)], axis=1)
    held = held.reshape(replicas, *value.shape)
    return jnp.stack(
        [lax.dynamic_index_in_dim(held, me ^ i, 0, keepdims=False) for i in range(replicas)]
    )


def local(
    tokens,
    cotangent,
    lengths,
    packing,
    attn_gain,
    w_query,
    w_key_value,
    w_out,
    mlp_gain,
    w_gate_up,
    w_down,
):
    ntok, width = tokens.shape
    total = packing.shape[1]
    groups = total // ntok
    shard = w_query.shape[0]
    replicas = lax.axis_size("replica")
    rows = shard // replicas
    kvl = KV_HEADS // groups
    hl = HEADS // groups
    qw = hl * HEAD_DIM
    kw = kvl * HEAD_DIM
    qkvw = qw + 2 * kw
    ff = w_gate_up.shape[2]
    ffs = ff // groups
    me_r = lax.axis_index("replica")
    line = Line(groups)

    def own_rows(value):
        return lax.dynamic_slice_in_dim(value, me_r * rows, rows)

    def over_plane(value):
        return lax.all_gather(value, "replica", axis=0)

    wq_rows = own_rows(w_query).reshape(rows, groups, qw)
    wkv_rows = own_rows(w_key_value).reshape(rows, 2, groups, kw)
    wkv_rows = wkv_rows.transpose(0, 2, 1, 3).reshape(rows, groups, 2 * kw)
    qkv_rows = jnp.concatenate([wq_rows, wkv_rows], axis=2)
    ffr = ffs // replicas
    gu_cols = []
    for k in range(groups):
        first = (line.me ^ k) * ffs + me_r * ffr
        part = lax.dynamic_slice(w_gate_up, (0, 0, first), (shard, 2, ffr))
        gu_cols.append(jnp.concatenate([part[:, 0], part[:, 1]], axis=1))
    gu_cols = jnp.stack(gu_cols)
    out_cols = lax.dynamic_slice_in_dim(w_out, me_r * (width // replicas), width // replicas, 1)

    w_qkv = line.exchange([line.at(qkv_rows, k, 1) for k in range(groups)])
    gains = jnp.stack([attn_gain, mlp_gain])
    gains = jnp.concatenate(line.ordered(line.exchange([gains] * groups)), axis=1)
    gain1, gain2 = gains[0], gains[1]
    w_out_cols = line.exchange([out_cols] * groups)
    x_hops = line.gather(tokens, (), 1)
    x_came = [part[1] for part in x_hops]
    w_qkv, w_out_cols[1:], x_came = after((w_qkv, w_out_cols[1:], x_came), gu_cols)
    x_hops = [[tokens, part] for part in x_came]
    seats = jnp.arange(total, dtype=jnp.int32)
    _, position = stream_meta(lengths[0], seats)
    start = (seats - position)[:, None]
    angles = position.astype(F32)[:, None] * frequencies(HEAD_DIM)[None, :]
    copies = 128 // HEAD_DIM
    cosine = jnp.tile(jnp.cos(angles), (1, 2 * copies))
    sine = jnp.sin(angles)
    sine = jnp.tile(jnp.concatenate([-sine, sine], axis=1), (1, copies))
    seat = packing.reshape(groups, ntok)
    seat = jnp.concatenate([line.at(seat, k) for k in range(groups)])
    place = (seat[None, :] == seats[:, None]).astype(BF16)
    w_qkv = over_plane(jnp.stack(line.ordered(w_qkv)))
    w_qkv = jnp.swapaxes(w_qkv, 0, 1).reshape(width, qkvw)
    x_slots = line.gather(tokens, (), 0, x_hops)
    x_last = [part[-1] for part in line.last]
    w_out_cols = over_plane(jnp.concatenate(w_out_cols))
    gu_cols = after(gu_cols, x_last)
    gu_cols = line.exchange([gu_cols[k] for k in range(groups)])
    dy_hops = line.gather(cotangent, (x_last,), 1)

    def normed(value):
        value = value.astype(F32)
        return (value * inverse_rms(value) * gain1).astype(BF16)

    normed1 = jnp.concatenate([normed(value) for value in x_slots])
    normed1 = dot(place, normed1, ((1,), (0,))).astype(BF16)
    qkv = dot(normed1, w_qkv, ((1,), (0,)))
    q_rot, k_rot, values, attended, lse, attended_low = attention_forward(
        hl, kvl, qkv, cosine, sine, start, place
    )

    def cut(value):
        return [value[k * ntok : (k + 1) * ntok] for k in range(groups)]

    dy_near = dy_hops
    attended_low = after(attended_low, [part[1] for part in dy_hops])
    own_attended = line.exchange(cut(attended_low))
    w_gu = over_plane(jnp.concatenate(line.ordered(after(gu_cols, attended_low))))
    x_own = tokens.astype(F32)
    own_attended_all = jnp.concatenate(own_attended, axis=1)
    h1 = lax.dot_general(own_attended_all, w_out_cols, (((1,), (1,)), ((), ())), preferred_element_type=F32)
    h1 = x_own + h1.reshape(ntok, width)
    inv2 = inverse_rms(h1)
    unit2 = h1 * inv2
    normed2 = (unit2 * gain2).astype(BF16)
    n2_near = line.gather(normed2, (), 1)
    dy_hops = line.gather(cotangent, (None, own_attended[1:]), 2, dy_hops)
    near_parts = [line.near(n2_near), line.near(dy_near)]

    half = groups // 2
    if half > 2:
        n2, dy = line.gather(normed2, (), 0, n2_near), line.gather(cotangent, (), 0, dy_hops)
        near_parts = [jnp.concatenate(part[:half]) for part in (n2, dy)]
    near = feed_forward(*near_parts, w_gu, w_down, HEAVY)
    if half == 2:
        n2 = line.gather(normed2, (None, None, near[3]), 0, n2_near)
        dy_hops = line.gather(cotangent, (None, None, n2_near), 3, dy_hops)
        for part, last in zip(dy_hops, after([part[-1] for part in dy_hops], near[3])):
            part[-1] = last
        dy = line.gather(cotangent, (), 0, dy_hops)
    n2_parts = [near_parts[0], jnp.concatenate(n2[half:])]
    dy_parts = [near_parts[1], jnp.concatenate(dy[half:])]
    n2_parts[1] = after(n2_parts[1], near[3])
    far = feed_forward(n2_parts[1], dy_parts[1], w_gu, w_down, LIGHT)
    grad_n2 = line.exchange(cut(near[3])[:half] + cut(far[3])[:half])

    def sum_plane(value):
        return lax.psum_scatter(value, "replica", scatter_dimension=0)

    hidden = [near[0], far[0]]
    down_grad, down_done = weight_gradient(hidden, [dy_parts], groups, replicas, False)
    n2_parts[0] = after(n2_parts[0], down_done)
    gu_grad, gu_done = weight_gradient(
        n2_parts, [[near[1], far[1]], [near[2], far[2]]], groups, replicas, True
    )
    down_grad = sum_plane(down_grad.reshape(replicas, ffs // replicas, width))
    gu_grad = gu_grad.reshape(replicas, groups * rows, 2 * ffs)
    gu_grad = sum_plane(gu_grad).reshape(groups, rows, 2 * ffs)

    grad_n2 = after(grad_n2, gu_done, cost=HEAVY)
    grad_n2 = sum([part.astype(F32) for part in grad_n2])
    gain2_grad = jnp.sum(grad_n2 * unit2, axis=0)
    grad_h1 = cotangent.astype(F32) + rms_norm_backward(grad_n2, unit2, inv2, gain2)
    grad_attn = grad_h1.astype(BF16)
    grad_heads = lax.dot_general(
        grad_attn.reshape(ntok, replicas, width // replicas),
        w_out_cols,
        (((1, 2), (0, 2)), ((), ())),
        preferred_element_type=F32,
    ).astype(BF16)
    heads_there = grad_heads
    grad_heads = line.exchange([grad_heads[:, k * qw : (k + 1) * qw] for k in range(groups)])
    grad_heads = jnp.concatenate(grad_heads)
    ga_hops = line.gather(grad_attn, (grad_heads,), 1)
    grad_qkv, own_qkv = attention_backward(
        hl, kvl, q_rot, k_rot, values, attended, lse, grad_heads, cosine, sine, start, place
    )
    down = [dot(after(part, own_qkv), w_down, ((1,), (0,))).astype(BF16) for part in hidden]
    down = cut(down[0])[:half] + cut(down[1])[:half]
    own_qkv = after(own_qkv, [part[1] for part in ga_hops])
    qkv_grad = dot(normed1, grad_qkv, ((0,), (0,))).astype(BF16)
    grad_n1 = dot(own_qkv, w_qkv, ((1,), (1,))).astype(BF16)

    def by_group(value):
        return line.exchange([line.at(value, k) for k in range(groups)])

    qkv_grad = qkv_grad.reshape(groups, replicas, rows, qkvw).transpose(1, 2, 0, 3)
    qkv_grad = qkv_grad.reshape(replicas, rows, groups * qkvw)
    n1_slots, n1_hops = cut(grad_n1), []
    for i in range(groups - 1):
        came = n1_hops[-1] if n1_hops else None
        gate = [part[-1] for part in ga_hops] if i else ()
        n1_hops.append(line.scatter_hop(n1_slots, came, groups - 1 - i, gate))
        if i + 2 < groups:
            gates = [None] * (i + 1) + [came if i else own_qkv]
            ga_hops = line.gather(grad_attn, gates, i + 2, ga_hops)
    gu_grad, down_grad, qkv_grad = after((gu_grad, down_grad, qkv_grad), n1_hops[0])
    qkv_grad = sum_plane(qkv_grad)
    down_grad = over_plane(down_grad).reshape(ffs, width)
    grad_n1 = sum(part.astype(F32) for part in (n1_slots[0], *n1_hops[-1]))
    grad_attn_all = line.gather(grad_attn, (), 0, ga_hops)
    inv1 = inverse_rms(x_own)
    unit1 = x_own * inv1
    gain1_grad = jnp.sum(grad_n1 * unit1, axis=0)
    x_grad = (grad_h1 + rms_norm_backward(grad_n1, unit1, inv1, gain1)).astype(BF16)

    grad_attn_all = jnp.concatenate(after(grad_attn_all, grad_n1))
    out_grad = dot(attended_low, grad_attn_all, ((0,), (0,))).astype(BF16)
    gain_grads = jnp.stack([gain1_grad, gain2_grad]).reshape(2, groups, replicas, rows)
    gain_grads = gain_grads.transpose(2, 3, 1, 0).astype(BF16)
    gain_grads = jnp.pad(gain_grads, ((0, 0), (0, 0), (0, 0), (0, 128 - 2)))
    out_grad = out_grad.reshape(replicas, rows, width)
    gain_grads = gain_grads.reshape(replicas, rows, groups * 128)
    out_grad = jnp.concatenate([out_grad, gain_grads], axis=2)
    gu_grad = by_group(after(gu_grad, n1_hops[-2], out_grad))
    out_grad = sum_plane(after(out_grad, down_grad, qkv_grad))
    y_hops = []
    for hop in range(groups - 1, 0, -1):
        gate = () if y_hops else gu_grad[1:]
        y_hops.append(line.scatter_hop(down, y_hops[-1] if y_hops else None, hop, gate))
    mixed = (h1 + sum(part.astype(F32) for part in (down[0], *y_hops[-1]))).astype(BF16)

    gu_grad = line.ordered(gu_grad)
    gu_grad = jnp.concatenate([part.reshape(rows, 2, ffs) for part in gu_grad], axis=2)
    gu_grad = over_plane(after(gu_grad, out_grad))

    grads = jnp.concatenate(
        [qkv_grad.reshape(rows, groups, qkvw), out_grad[:, width:].reshape(rows, groups, 128)], axis=2
    )
    grads = by_group(jnp.swapaxes(grads, 0, 1))
    gain_grads = sum([part[:, qkvw:].astype(F32) for part in grads]).astype(BF16)
    grads = line.ordered(grads)
    grads = [part[:, :qw] for part in grads] + [
        part[:, qw + j * kw : qw + (j + 1) * kw] for j in range(2) for part in grads
    ]
    grads = jnp.concatenate(grads + [out_grad[:, :width], gain_grads], axis=1)
    grads = gather_plane(grads, replicas, me_r)
    gu_grad = gu_grad.reshape(shard, 2, ff).astype(F32)
    down_grad = down_grad.astype(F32)
    grads = grads.reshape(shard, -1).astype(F32)
    q_grad = grads[:, :width]
    kv_grad = grads[:, width : width + 2 * groups * kw].reshape(shard, 2, groups * kw)
    out_grad = grads[:, width + 2 * groups * kw : 2 * width + 2 * groups * kw]
    gain_grads = grads[:, -128:]
    return (
        mixed,
        x_grad,
        gain_grads[:, 0],
        q_grad,
        kv_grad,
        out_grad,
        gain_grads[:, 1],
        gu_grad,
        down_grad,
    )


def solution(mesh):
    rows = P(("replica", "group"), None)
    flat, two, three = P("group"), P("group", None), P("group", None, None)
    return jax.shard_map(
        local,
        mesh=mesh,
        in_specs=(
            rows,
            rows,
            P("replica", None),
            P("replica", None),
            flat,
            two,
            three,
            two,
            flat,
            three,
            two,
        ),
        out_specs=(rows, rows, flat, two, three, two, flat, three, two),
        check_vma=False,
    )
```
